32 devices in a mesh: vel: 8 (over z, core), space: 4 (over y, x).
Axes of the slice: x: 2, y: 2, z: 4, core: 2. Of those that a mesh axis runs over, the one named last changes fastest.
Arguments:
- deviation: bfloat16 [8, 8, 16, 13824], P('space', None, None, 'vel'), may hold values from -6 to 6
- collision: bfloat16 [13824, 13824], P('vel'), may hold values from -0.0546875 to 0.0546875
- vel_order: int32 [13824], P('vel'), may hold values from 0 to 13823, each once
- inflow_value: bfloat16 [13824], P('vel'), may hold values from -6 to 6
- wall_flag: int32 [8, 8, 16], P('space'), may hold values 0 or 1
- inflow_flag: int32 [8, 8, 16], P('space'), may hold values 0 or 1
Outputs:
- final_deviation: bfloat16 [8, 8, 16, 13824], P('space', None, None, 'vel')
- density: float32 [8, 8, 16], P('space')
The draws below stay inside these ranges and needn't reach their ends.
All inputs are finite; a program needn't handle non-finite values. No bound on the sum of `wall_flag` or of `inflow_flag` on one device may be relied on, other than what follows from the above.
Results may differ from the reference program's by a relative error of at most 0.0047.
Values may be sent and summed in bfloat16 or wider, within the bound.
No kernel may reach another device: no remote copies, remote signals or barrier semaphores. Data moves between devices by JAX's collectives and lax.ppermute only.
A program may use at most 192 MiB of HBM per device.

```python
import jax
import jax.numpy as jnp
from jax import lax

NV = 24
V = 13824
GY = 8
GZ = 16
ITERS = 2
GX = 8


def with_ends(result, rng, least, top_value):
    shape = result.shape
    place = [jax.random.randint(jax.random.fold_in(rng, axis), (), 0, shape[axis]) for axis in range(len(shape))]
    result = result.at[tuple(place)].set(least)
    longest = shape.index(max(shape))
    place[longest] = (place[longest] + 1) % shape[longest]
    return result.at[tuple(place)].set(top_value)


def steps_of(rng, dims, shards, least, top_value):
    factor_of = 1.0
    for axis_at, blocks in shards:
        heights = jax.random.uniform(jax.random.fold_in(jax.random.fold_in(rng, 6), axis_at), (blocks,), jnp.float32, least / len(shards), top_value / len(shards))
        factor_of = factor_of * jnp.repeat(jnp.exp(heights), dims[axis_at] // blocks).reshape((-1,) + (1,) * (len(dims) - 1 - axis_at))
    return factor_of


def normal_values(stream_key, dims, spread, limit, shards=(), held_as=jnp.bfloat16):
    array = jax.random.normal(stream_key, dims, jnp.float32) * spread
    if len(shards) > 0:
        array = steps_of(stream_key, dims, shards, -0.22, 0.18) * array
    return jnp.clip(array, min=-limit, max=limit).astype(held_as)


def setup_inputs(seed: int = 0) -> dict:
    seeds = jax.random.split(jax.random.key(seed), 7)
    deviation = normal_values(seeds[0], (GX, GY, GZ, V), 1.0, 6.0, ((0, 4), (3, 8)))
    collision = normal_values(seeds[1], (V, V), V ** -0.5, 0.0546875, ((0, 8),))
    vel_order = jax.random.permutation(seeds[2], V).astype(jnp.int32)
    inflow_value = normal_values(seeds[3], (V,), 1.0, 6.0, ((0, 8),))
    wall_flag = with_ends((jax.random.randint(seeds[4], (GX, GY, GZ), 0, 8) < 1).astype(jnp.int32), jax.random.fold_in(seeds[4], 1), 0, 1)
    inflow_flag = with_ends((jax.random.randint(seeds[5], (GX, GY, GZ), 0, 8) < 1).astype(jnp.int32), jax.random.fold_in(seeds[5], 1), 0, 1)
    return dict(deviation=deviation, collision=collision, vel_order=vel_order, inflow_value=inflow_value, wall_flag=wall_flag, inflow_flag=inflow_flag)


def speeds(vel_order):
    kx = vel_order // (NV * NV)
    ky = vel_order // NV % NV
    kz = vel_order % NV
    scale = 0.9 / (1.5 * (NV - 1))
    half = (NV - 1) / 2.0
    return [(k.astype(jnp.float32) - half) * scale for k in (kx, ky, kz)]

def stream(relaxed, speed_list):
    field = relaxed.astype(jnp.float32)
    total = field
    for axis_num in range(3):
        speed = speed_list[axis_num]
        back = field - jnp.roll(field, 1, axis=axis_num)
        fore = jnp.roll(field, -1, axis=axis_num) - field
        total = total - jnp.where(speed > 0, speed * back, speed * fore)
    return total

def reference(deviation, collision, vel_order, inflow_value, wall_flag, inflow_flag):
    speed_list = speeds(vel_order)
    state = deviation
    shape = state.shape
    for step in range(ITERS):
        flat = state.reshape(-1, shape[3])
        image = lax.dot_general(flat, collision, (((1,), (1,)), ((), ())), preferred_element_type=jnp.float32)
        relaxed = (0.5 * flat.astype(jnp.float32) + 0.5 * image).astype(jnp.bfloat16).reshape(shape)
        read = stream(relaxed, speed_list)
        read = jnp.where(inflow_flag[..., None] == 1, inflow_value.astype(jnp.float32), read)
        read = jnp.where(wall_flag[..., None] == 1, 0.0, read)
        state = read.astype(jnp.bfloat16)
    density = lax.optimization_barrier(jnp.sum(state.astype(jnp.float32), axis=3)) / jnp.sqrt(jnp.float32(V))
    return (state, density)
```

```python
import functools

import jax
import jax.numpy as jnp
from jax import lax
from jax.experimental import pallas as pl
from jax.experimental.pallas import tpu as pltpu
from jax.sharding import PartitionSpec as P

NV = 24
V = 13824
ITERS = 2
LANES = 128
HALF = LANES // 2
VMEM_LIMIT = 40 * 1024 * 1024


def speeds(vel_order):
    kx = vel_order // (NV * NV)
    ky = vel_order // NV % NV
    kz = vel_order % NV
    scale = 0.9 / (1.5 * (NV - 1))
    half = (NV - 1) / 2.0
    return [(k.astype(jnp.float32) - half) * scale for k in (kx, ky, kz)]


def ring(axis):
    count = lax.axis_size(axis)
    forward = [(i, (i + 1) % count) for i in range(count)]
    return forward, [(target, source) for source, target in forward]


def plain_step(state, collision, speed_list, inflow_value, wall_flag, inflow_flag):
    shape = state.shape
    cells = shape[0] * shape[1] * shape[2]
    local_vel = shape[3]
    flat = state.reshape(cells, local_vel)
    gathered = lax.all_gather(flat, "vel")
    gathered = gathered.transpose(1, 0, 2).reshape(cells, collision.shape[1])
    image = lax.dot_general(
        gathered, collision, (((1,), (1,)), ((), ())), preferred_element_type=jnp.float32
    )
    relaxed = (0.5 * flat.astype(jnp.float32) + 0.5 * image).astype(jnp.bfloat16).reshape(shape)
    forward, backward = ring("space")
    low = lax.ppermute(relaxed[-1:], "space", forward)
    high = lax.ppermute(relaxed[:1], "space", backward)
    padded = jnp.concatenate([low, relaxed, high], axis=0).astype(jnp.float32)
    field = padded[1:-1]
    total = field
    for axis, speed in enumerate(speed_list):
        if axis == 0:
            lower, upper = padded[:-2], padded[2:]
        else:
            lower, upper = jnp.roll(field, 1, axis=axis), jnp.roll(field, -1, axis=axis)
        total = total - jnp.where(speed > 0, speed * (field - lower), speed * (upper - field))
    total = jnp.where(inflow_flag[..., None] == 1, inflow_value.astype(jnp.float32), total)
    total = jnp.where(wall_flag[..., None] == 1, 0.0, total)
    return total.astype(jnp.bfloat16)


def plain(deviation, collision, vel_order, inflow_value, wall_flag, inflow_flag):
    state = deviation
    for _ in range(ITERS):
        state = plain_step(
            state, collision, speeds(vel_order), inflow_value, wall_flag, inflow_flag
        )
    partial_sum = jnp.sum(state.astype(jnp.float32), axis=3)
    return state, lax.psum(partial_sum, "vel") / jnp.sqrt(jnp.float32(V))


def vmem(count):
    return [pl.BlockSpec(memory_space=pltpu.VMEM)] * count


def params():
    return pltpu.CompilerParams(vmem_limit_bytes=VMEM_LIMIT)


def packed_rows(cells, local):
    return cells * local // LANES


def rows_at(start, size):
    return pl.ds(pl.multiple_of(start, 16), size)


def pack_kernel(runs, deviation_ref, *outs):
    planes, _, depth, local = deviation_ref.shape
    full = local // LANES
    for ys, out_ref in zip(runs, outs):
        cells = planes * len(ys) * depth
        half = cells // 2
        for x in range(planes):
            for i, y in enumerate(ys):
                at = (x * len(ys) + i) * depth
                for t in range(full):
                    out_ref[t * cells + at : t * cells + at + depth, :] = deviation_ref[
                        x, y, :, t * LANES : (t + 1) * LANES
                    ]
                side = 0 if at < half else 1
                at = full * cells + at - side * half
                out_ref[at : at + depth, side * HALF : (side + 1) * HALF] = deviation_ref[
                    x, y, :, full * LANES : local
                ]


def pack(deviation, runs):
    planes, _, depth, local = deviation.shape
    return pl.pallas_call(
        functools.partial(pack_kernel, runs),
        out_shape=[
            jax.ShapeDtypeStruct(
                (packed_rows(planes * len(ys) * depth, local), LANES), jnp.bfloat16
            )
            for ys in runs
        ],
        in_specs=vmem(1),
        out_specs=vmem(len(runs)),
        compiler_params=params(),
        name="pack",
    )(deviation)


def row_block(rows):
    return max(b for b in range(16, 577, 16) if rows % b == 0)


def matmul_kernel(count, cells, local, planes, has_acc, last, buffers, chips_ref, core_ref, *refs):
    refs = list(refs)
    pairs = [(refs.pop(0), refs.pop(0)) for _ in range(count)]
    collision_ref = refs.pop(0)
    acc_ref = refs.pop(0) if has_acc else None
    state_ref = refs.pop(0) if last else None
    outs = [refs.pop(0) for _ in range(planes if last else 1)]
    buffer_ref, sems, whole_ref, total_ref = refs
    total_ref = total_ref if last else outs[0]
    rows = buffer_ref.shape[1]
    blocks = local // rows
    steps = blocks * count
    full = local // LANES
    half = cells // 2
    width = 2 * local

    def copy(n):
        columns = pl.ds(pl.multiple_of(chips_ref[n // blocks] * width, LANES), width)
        return pltpu.make_async_copy(
            collision_ref.at[rows_at(n % blocks * rows, rows), columns],
            buffer_ref.at[n % buffers],
            sems.at[n % buffers],
        )

    for n in range(min(buffers - 1, steps)):
        copy(n).start()

    first_core = core_ref[0] == 0
    for k, (own_ref, other_ref) in enumerate(pairs):

        def tile(t, size=cells):
            own, other = own_ref[t * cells : t * cells + size], other_ref[t * cells : t * cells + size]
            return jnp.where(first_core, own, other), jnp.where(first_core, other, own)

        tiles = [tile(t) for t in range(full)]
        ends = tile(full, half)
        ends = [jnp.concatenate([e[:, :HALF], e[:, HALF:]], axis=0) for e in ends]
        for t in range(full):
            whole_ref[k, 0:cells, t * LANES : (t + 1) * LANES] = tiles[t][0]
        middle = jnp.concatenate([ends[0], tiles[0][1][:, :HALF]], axis=1)
        whole_ref[k, 0:cells, full * LANES : (full + 1) * LANES] = middle
        for t in range(full):
            right = tiles[t + 1][1][:, :HALF] if t + 1 < full else ends[1]
            both = jnp.concatenate([tiles[t][1][:, HALF:], right], axis=1)
            at = (full + 1 + t) * LANES
            whole_ref[k, 0:cells, at : at + LANES] = both

    total_ref[...] = acc_ref[...] if has_acc else jnp.zeros_like(total_ref)

    def step(n, carry):
        @pl.when(n + buffers - 1 < steps)
        def _():
            copy(n + buffers - 1).start()

        copy(n).wait()
        total_ref[rows_at(n % blocks * rows, rows), :] += lax.dot_general(
            buffer_ref[n % buffers],
            whole_ref[n // blocks],
            (((1,), (1,)), ((), ())),
            preferred_element_type=jnp.float32,
        )
        return carry

    lax.fori_loop(0, steps, step, 0)

    if last:
        size = cells // planes

        def relax(state, image):
            return (0.5 * state.astype(jnp.float32) + 0.5 * image).astype(jnp.bfloat16)

        def relax_tile(t, carry):
            image = total_ref[pl.ds(pl.multiple_of(t * LANES, LANES), LANES), :].T[0:cells, :]
            relaxed = relax(state_ref[rows_at(t * cells, cells), :], image)
            for x in range(planes):
                outs[x][rows_at(t * size, size), :] = relaxed[x * size : (x + 1) * size, :]
            return carry

        lax.fori_loop(0, full, relax_tile, 0)
        image = total_ref[full * LANES : local, :].T[0:cells, :]
        end = state_ref[full * cells : full * cells + half, :]
        relaxed = relax(jnp.concatenate([end[:, :HALF], end[:, HALF:]], axis=0), image)
        for x in range(planes):
            outs[x][full * size : (full + 1) * size, 0:HALF] = relaxed[x * size : (x + 1) * size, :]
            outs[x][full * size : (full + 1) * size, HALF:LANES] = jnp.zeros((size, HALF), jnp.bfloat16)


def matmul(pairs, chips, core, collision, cells, acc=None, state=None, planes=0):
    local = collision.shape[0]
    rows = row_block(local)
    buffers = 3
    count = len(pairs)
    padded = -(-cells // LANES) * LANES
    last = state is not None
    operands = [a for pair in pairs for a in pair] + [collision]
    in_specs = vmem(2 * count) + [pl.BlockSpec(memory_space=pl.ANY)]
    for extra in (acc, state):
        if extra is not None:
            operands.append(extra)
            in_specs += vmem(1)
    if last:
        tiles = local // LANES + 1
        out_shape = [
            jax.ShapeDtypeStruct((tiles * cells // planes, LANES), jnp.bfloat16)
        ] * planes
    else:
        out_shape = [jax.ShapeDtypeStruct((local, padded), jnp.float32)]
    scalar = pl.BlockSpec(memory_space=pltpu.SMEM)
    return pl.pallas_call(
        functools.partial(
            matmul_kernel, count, cells, local, planes, acc is not None, last, buffers
        ),
        out_shape=out_shape,
        in_specs=[scalar, scalar] + in_specs,
        out_specs=vmem(len(out_shape)),
        scratch_shapes=[
            pltpu.VMEM((buffers, rows, 2 * local), jnp.bfloat16),
            pltpu.SemaphoreType.DMA((buffers,)),
            pltpu.VMEM((count, padded, 2 * local), jnp.bfloat16),
            pltpu.VMEM((local, padded) if last else (8, LANES), jnp.float32),
        ],
        compiler_params=params(),
        cost_estimate=pl.CostEstimate(
            flops=4 * count * local * local * 256,
            bytes_accessed=4 * count * local * local,
            transcendentals=0,
        ),
        name="collide",
    )(jnp.stack(chips).astype(jnp.int32), core.astype(jnp.int32)[None], *operands)


def stream_kernel(ys, where_is, planes, depth, final, sizes, speed_ref, inflow_ref, code_ref, *refs):
    refs = list(refs)
    chunks = [[refs.pop(0) for _ in range(planes + 2)] for _ in sizes]
    out_ref = refs.pop(0)
    height = len(where_is)
    full = speed_ref.shape[0] - 1
    cells = planes * len(ys) * depth
    half = cells // 2

    def tile(t, tail):
        def plane(x, y):
            chunk, at = where_is[y % height]
            ref = chunks[chunk][x + 1]
            return ref[rows_at(t * sizes[chunk] + at * depth, depth), :].astype(jnp.float32)

        speed = [speed_ref[t, d : d + 1, :] for d in range(3)]
        size = [jnp.abs(s) for s in speed]
        up = [s > 0 for s in speed]
        inflow = inflow_ref[t, 0:1, :].astype(jnp.float32)
        for x in range(planes):
            for i, y in enumerate(ys):
                field = plane(x, y)
                total = field
                for d in range(3):
                    if d == 0:
                        lower, upper = plane(x - 1, y), plane(x + 1, y)
                    elif d == 1:
                        lower, upper = plane(x, y - 1), plane(x, y + 1)
                    else:
                        lower = pltpu.roll(field, 1, 0)
                        upper = pltpu.roll(field, depth - 1, 0)
                    near = jnp.where(up[d], lower, upper)
                    total = total - size[d] * (field - near)
                at = (x * height + y) * depth
                code = code_ref[at : at + depth, :]
                total = jnp.where(code == 0, total, jnp.where(code == 1, inflow, 0.0))
                total = total.astype(jnp.bfloat16)
                at = (x * len(ys) + i) * depth
                if final:
                    wide = total.astype(jnp.float32)
                    if tail:
                        out_ref[at : at + depth, full * LANES : full * LANES + HALF] = total[:, :HALF]
                        lane = lax.broadcasted_iota(jnp.int32, wide.shape, 1)
                        wide = jnp.where(lane < HALF, wide, 0.0)
                        summed = refs[1][at : at + depth, :] + wide
                        refs[0][at : at + depth, :] = jnp.sum(summed, axis=1, keepdims=True)
                    else:
                        lanes = pl.ds(pl.multiple_of(t * LANES, LANES), LANES)
                        out_ref[at : at + depth, lanes] = total
                        refs[1][at : at + depth, :] += wide
                elif tail:
                    side = 0 if at < half else 1
                    at = full * cells + at - side * half
                    out_ref[at : at + depth, side * HALF : (side + 1) * HALF] = total[:, :HALF]
                else:
                    out_ref[rows_at(t * cells + at, depth), :] = total

    if final:
        refs[1][...] = jnp.zeros_like(refs[1])

    def body(t, carry):
        tile(t, False)
        return carry

    lax.fori_loop(0, full, body, 0)
    tile(full, True)


def stream(ys, chunks, where_is, speed, inflow, code, planes, depth, local, final):
    used = sorted({where_is[(y + d) % len(where_is)][0] for y in ys for d in (-1, 0, 1)})
    where_is = [(used.index(c) if c in used else None, at) for c, at in where_is]
    operands = [a for c in used for a in chunks[c]]
    tiles = local // LANES + 1
    sizes = tuple(chunks[c][0].shape[0] // tiles for c in used)
    cells = planes * len(ys) * depth
    scratch = []
    if final:
        out_shape = [
            jax.ShapeDtypeStruct((cells, local), jnp.bfloat16),
            jax.ShapeDtypeStruct((cells, 1), jnp.float32),
        ]
        scratch = [pltpu.VMEM((cells, LANES), jnp.float32)]
    else:
        out_shape = [jax.ShapeDtypeStruct((packed_rows(cells, local), LANES), jnp.bfloat16)]
    return pl.pallas_call(
        functools.partial(stream_kernel, tuple(ys), tuple(where_is), planes, depth, final, sizes),
        out_shape=out_shape,
        in_specs=vmem(3 + len(operands)),
        out_specs=vmem(len(out_shape)),
        scratch_shapes=scratch,
        compiler_params=params(),
        cost_estimate=pl.CostEstimate(
            flops=40 * cells * local, bytes_accessed=12 * cells * local, transcendentals=0
        ),
        name="stream",
    )(speed, inflow, code, *operands)


def line_perm(pairs):
    return [(2 * a + c, 2 * b + c) for a, b in pairs for c in range(2)]


def other_core(block):
    return lax.ppermute(block, "vel", [(i, i ^ 1) for i in range(8)])


def line_sum(part):
    part = part + other_core(part)
    for mask in (1, 2):
        perm = line_perm([(a, a ^ mask) for a in range(4)])
        part = part + lax.ppermute(part, "vel", perm)
    return part


def line_gather(own, chip):
    far = lax.ppermute(own, "vel", line_perm([(a, a ^ 3) for a in range(4)]))
    near = lax.ppermute(own, "vel", line_perm([(a, a ^ 1) for a in range(4)]))
    middle = (chip == 1) | (chip == 2)
    relayed = jnp.where(middle, far, own)
    rest = lax.ppermute(relayed, "vel", line_perm([(0, 2), (3, 1), (2, 3), (1, 0)]))
    return [(block, other_core(block)) for block in (own, near, far, rest)]


def split_rows(height, sizes, turn):
    assert sum(sizes) == height
    runs, at = [], turn
    for size in sizes:
        runs.append(tuple((at + i) % height for i in range(size)))
        at += size
    return runs


PLANS = (((8,), 0), ((8,), 0), ((8,), 0))


def line(deviation, collision, vel_order, inflow_value, wall_flag, inflow_flag):
    planes, height, depth, local = deviation.shape
    index = lax.axis_index("vel")
    chip, core = index // 2, index % 2
    order = [chip, chip ^ 1, chip ^ 3, chip ^ 2]
    tiles = local // LANES + 1

    def by_tile(rows):
        rows = jnp.pad(rows, ((0, 0), (0, tiles * LANES - local)))
        return rows.reshape(-1, tiles, LANES).transpose(1, 0, 2)

    speed = by_tile(jnp.stack(speeds(vel_order)))
    inflow = by_tile(inflow_value[None, :].astype(jnp.float32))
    code = jnp.where(wall_flag == 1, 2, inflow_flag).reshape(-1, 1)
    forward, backward = ring("space")

    runs = split_rows(height, *PLANS[0])
    states = pack(deviation, runs)
    for step in range(ITERS):
        chunks, where_is = [], [None] * height
        for number, (ys, own) in enumerate(zip(runs, states)):
            cells = planes * len(ys) * depth
            blocks = line_gather(own, chip)
            acc = matmul(blocks[:3], order[:3], core, collision, cells)[0]
            relaxed = matmul(
                blocks[3:], order[3:], core, collision, cells, acc=acc, state=own, planes=planes
            )
            low = lax.ppermute(relaxed[-1], "space", forward)
            high = lax.ppermute(relaxed[0], "space", backward)
            chunks.append([low, *relaxed, high])
            for at, y in enumerate(ys):
                where_is[y] = (number, at)
        final = step == ITERS - 1
        runs = split_rows(height, *PLANS[step + 1])
        results = [
            stream(ys, chunks, where_is, speed, inflow, code, planes, depth, local, final)
            for ys in runs
        ]
        states = [r[0] for r in results]
    position = {y: (k, i) for k, ys in enumerate(runs) for i, y in enumerate(ys)}

    def assemble(arrays, width):
        arrays = [a.reshape(planes, -1, depth, width) for a in arrays]
        if len(arrays) == 1:
            return arrays[0]
        parts = [arrays[k][:, i : i + 1] for k, i in map(position.get, range(height))]
        return jnp.concatenate(parts, axis=1)

    state = assemble(states, local)
    partial_sum = assemble([r[1] for r in results], 1)[..., 0]
    return state, line_sum(partial_sum) / jnp.sqrt(jnp.float32(V))


def shards(deviation, collision, *rest):
    planes, _, depth, local = deviation.shape
    fits = local % LANES == HALF and planes % 2 == 0 and depth % 16 == 0
    body = line if lax.axis_size("vel") == 8 and fits else plain
    return body(deviation, collision, *rest)


def solution(mesh):
    placed = (
        P("space", None, None, "vel"),
        P("vel", None),
        P("vel"),
        P("vel"),
        P("space", None, None),
        P("space", None, None),
    )
    return jax.shard_map(
        shards,
        mesh=mesh,
        in_specs=placed,
        out_specs=(P("space", None, None, "vel"), P("space", None, None)),
        check_vma=False,
    )
```

```python
import functools

import jax
import jax.numpy as jnp
from jax import lax
from jax.experimental import pallas as pl
from jax.experimental.pallas import tpu as pltpu
from jax.sharding import PartitionSpec as P

NV = 24
V = 13824
ITERS = 2
LANES = 128
HALF = LANES // 2
COST = 1024
STREAM_COST = 1024
VMEM_LIMIT = 36 * 1024 * 1024
BUFFERS = 3


def speeds(vel_order):
    kx = vel_order // (NV * NV)
    ky = vel_order // NV % NV
    kz = vel_order % NV
    scale = 0.9 / (1.5 * (NV - 1))
    half = (NV - 1) / 2.0
    return [(k.astype(jnp.float32) - half) * scale for k in (kx, ky, kz)]


def ring(axis):
    count = lax.axis_size(axis)
    forward = [(i, (i + 1) % count) for i in range(count)]
    return forward, [(target, source) for source, target in forward]


def plain_step(state, collision, speed_list, inflow_value, wall_flag, inflow_flag):
    shape = state.shape
    cells = shape[0] * shape[1] * shape[2]
    local_vel = shape[3]
    flat = state.reshape(cells, local_vel)
    gathered = lax.all_gather(flat, "vel")
    gathered = gathered.transpose(1, 0, 2).reshape(cells, collision.shape[1])
    image = lax.dot_general(
        gathered, collision, (((1,), (1,)), ((), ())), preferred_element_type=jnp.float32
    )
    relaxed = (0.5 * flat.astype(jnp.float32) + 0.5 * image).astype(jnp.bfloat16).reshape(shape)
    forward, backward = ring("space")
    low = lax.ppermute(relaxed[-1:], "space", forward)
    high = lax.ppermute(relaxed[:1], "space", backward)
    padded = jnp.concatenate([low, relaxed, high], axis=0).astype(jnp.float32)
    field = padded[1:-1]
    total = field
    for axis, speed in enumerate(speed_list):
        if axis == 0:
            lower, upper = padded[:-2], padded[2:]
        else:
            lower, upper = jnp.roll(field, 1, axis=axis), jnp.roll(field, -1, axis=axis)
        total = total - jnp.where(speed > 0, speed * (field - lower), speed * (upper - field))
    total = jnp.where(inflow_flag[..., None] == 1, inflow_value.astype(jnp.float32), total)
    total = jnp.where(wall_flag[..., None] == 1, 0.0, total)
    return total.astype(jnp.bfloat16)


def plain(deviation, collision, vel_order, inflow_value, wall_flag, inflow_flag):
    state = deviation
    for _ in range(ITERS):
        state = plain_step(
            state, collision, speeds(vel_order), inflow_value, wall_flag, inflow_flag
        )
    partial_sum = jnp.sum(state.astype(jnp.float32), axis=3)
    return state, lax.psum(partial_sum, "vel") / jnp.sqrt(jnp.float32(V))


PARTS = (7,)


def vmem(count):
    return [pl.BlockSpec(memory_space=pltpu.VMEM)] * count


def params():
    return pltpu.CompilerParams(vmem_limit_bytes=VMEM_LIMIT)


def cost(size=COST):
    return pl.CostEstimate(flops=size, bytes_accessed=size, transcendentals=0)


def rows_at(start, size):
    return pl.ds(pl.multiple_of(start, 16), size)


def part_tiles(local):
    cuts = (0, *PARTS, local // LANES + 1)
    return list(zip(cuts[:-1], cuts[1:]))


def packed_rows(first, end, cells, local):
    return (end - first) * cells - (cells // 2 if end * LANES > local else 0)


def pack_kernel(deviation_ref, *outs):
    planes, height, depth, local = deviation_ref.shape
    cells = planes * height * depth
    half = cells // 2
    full = local // LANES
    for (first, end), out_ref in zip(part_tiles(local), outs):
        for x in range(planes):
            for y in range(height):
                at = (x * height + y) * depth
                for t in range(first, min(end, full)):
                    to = (t - first) * cells + at
                    out_ref[to : to + depth, :] = deviation_ref[
                        x, y, :, t * LANES : (t + 1) * LANES
                    ]
                if end > full:
                    side = 0 if at < half else 1
                    to = (full - first) * cells + at - side * half
                    out_ref[to : to + depth, side * HALF : (side + 1) * HALF] = deviation_ref[
                        x, y, :, full * LANES : local
                    ]


def pack(deviation):
    planes, height, depth, local = deviation.shape
    cells = planes * height * depth
    out_shape = [
        jax.ShapeDtypeStruct((packed_rows(*part, cells, local), LANES), jnp.bfloat16)
        for part in part_tiles(local)
    ]
    return pl.pallas_call(
        pack_kernel,
        out_shape=out_shape,
        in_specs=vmem(1),
        out_specs=vmem(len(out_shape)),
        compiler_params=params(),
        cost_estimate=cost(),
        name="pack",
    )(deviation)


def row_block(rows):
    return max(b for b in range(16, 577, 16) if rows % b == 0)


def unpack(own_ref, other_ref, first_core, whole_ref, k, cells, local):
    full = local // LANES
    half = cells // 2

    def tile(t, size=cells):
        own, other = own_ref[t * cells : t * cells + size], other_ref[t * cells : t * cells + size]
        return jnp.where(first_core, own, other), jnp.where(first_core, other, own)

    tiles = [tile(t) for t in range(full)]
    ends = tile(full, half)
    ends = [jnp.concatenate([e[:, :HALF], e[:, HALF:]], axis=0) for e in ends]
    for t in range(full):
        whole_ref[k, 0:cells, t * LANES : (t + 1) * LANES] = tiles[t][0]
    middle = jnp.concatenate([ends[0], tiles[0][1][:, :HALF]], axis=1)
    whole_ref[k, 0:cells, full * LANES : (full + 1) * LANES] = middle
    for t in range(full):
        right = tiles[t + 1][1][:, :HALF] if t + 1 < full else ends[1]
        both = jnp.concatenate([tiles[t][1][:, HALF:], right], axis=1)
        at = (full + 1 + t) * LANES
        whole_ref[k, 0:cells, at : at + LANES] = both


def matmul_kernel(
    count, pieces, cells, local, part, planes, has_acc, has_token, buffers, chips_ref, core_ref, *refs
):
    refs = list(refs)
    given = [[refs.pop(0) for _ in range(pieces)] for _ in range(2 * count)]
    collision_ref = refs.pop(0)
    acc_ref = refs.pop(0) if has_acc else None
    state_ref = refs.pop(0) if part else None
    if has_token:
        refs.pop(0)
    outs = [refs.pop(0) for _ in range(planes if part else 1)]
    if part:
        token_ref = refs.pop(0)
        token_ref[...] = jnp.zeros_like(token_ref)
    buffer_ref, sems, whole_ref, total_ref, load_sems, state_there = refs[:6]
    blocks_ref = refs[6:]
    total_ref = total_ref if part else outs[0]
    first, end = part or (0, local // LANES + 1)
    height = total_ref.shape[0]
    rows = buffer_ref.shape[1]
    blocks = height // rows
    steps = blocks * count
    width = 2 * local

    def copy(n):
        columns = pl.ds(pl.multiple_of(chips_ref[n // blocks] * width, LANES), width)
        return pltpu.make_async_copy(
            collision_ref.at[rows_at(first * LANES + n % blocks * rows, rows), columns],
            buffer_ref.at[n % buffers],
            sems.at[n % buffers],
        )

    def load(sources, target, number):
        copies, start = [], 0
        for i, source in enumerate(sources):
            here = pl.ds(start, source.shape[0])
            copies.append(
                pltpu.make_async_copy(source, target.at[here], load_sems.at[number * pieces + i])
            )
            start += source.shape[0]
        for one in copies:
            one.start()
        return copies

    def wait(copies):
        for one in copies:
            one.wait()

    loads = [load(sources, blocks_ref[i], i) for i, sources in enumerate(given)]
    for n in range(min(buffers - 1, steps)):
        copy(n).start()
    if has_acc:
        old = acc_ref.at[first * LANES : first * LANES + height, :]
        loads.append(load([old], total_ref, len(given)))
    if part:
        state_copy = load([state_ref], state_there, len(given) + 1)

    first_core = core_ref[0] == 0
    if not has_acc:
        total_ref[...] = jnp.zeros_like(total_ref)
    for k in range(count):
        wait(loads[2 * k] + loads[2 * k + 1])
        unpack(blocks_ref[2 * k], blocks_ref[2 * k + 1], first_core, whole_ref, k, cells, local)
    if has_acc:
        wait(loads[-1])

    def step(n, carry):
        @pl.when(n + buffers - 1 < steps)
        def _():
            copy(n + buffers - 1).start()

        copy(n).wait()
        total_ref[rows_at(n % blocks * rows, rows), :] += lax.dot_general(
            buffer_ref[n % buffers],
            whole_ref[n // blocks],
            (((1,), (1,)), ((), ())),
            preferred_element_type=jnp.float32,
        )
        return carry

    lax.fori_loop(0, steps, step, 0)

    if part:
        wait(state_copy)
        size = cells // planes
        whole_tiles = height // LANES

        def relax(t, state, image, lanes):
            relaxed = 0.5 * state.astype(jnp.float32) + 0.5 * image.T[0:cells, :]
            relaxed = relaxed.astype(jnp.bfloat16)
            for x in range(planes):
                outs[x][rows_at(t * size, size), 0:lanes] = relaxed[x * size : (x + 1) * size, :]

        def relax_tile(t, carry):
            image = total_ref[rows_at(t * LANES, LANES), :]
            relax(t, state_there[rows_at(t * cells, cells), :], image, LANES)
            return carry

        lax.fori_loop(0, whole_tiles, relax_tile, 0)
        if height % LANES:
            last = state_there[whole_tiles * cells :, :]
            state = jnp.concatenate([last[:, :HALF], last[:, HALF:]], axis=0)
            relax(whole_tiles, state, total_ref[whole_tiles * LANES :, :], HALF)
            for out_ref in outs:
                out_ref[whole_tiles * size :, HALF:LANES] = jnp.zeros((size, HALF), jnp.bfloat16)


def matmul(
    pairs,
    chips,
    core,
    collision,
    cells,
    acc=None,
    part=None,
    state=None,
    planes=0,
    token=None,
    size=COST,
):
    local = collision.shape[0]
    height = local
    if part:
        height = min(part[1] * LANES, local) - part[0] * LANES
    rows = row_block(height)
    buffers = BUFFERS
    count, pieces = len(pairs), len(pairs[0][0])
    padded = -(-cells // LANES) * LANES
    given = [a for pair in pairs for block in pair for a in block]
    operands = given + [collision] + [a for a in (acc, state, token) if a is not None]
    if part:
        shape = ((part[1] - part[0]) * cells // planes, LANES)
        out_shape = [jax.ShapeDtypeStruct(shape, jnp.bfloat16)] * planes
        out_shape.append(jax.ShapeDtypeStruct((8, LANES), jnp.float32))
    else:
        out_shape = [jax.ShapeDtypeStruct((local, padded), jnp.float32)]
    scalar = pl.BlockSpec(memory_space=pltpu.SMEM)
    small = (16, LANES)
    block = (packed_rows(0, local // LANES + 1, cells, local), LANES)
    return pl.pallas_call(
        functools.partial(
            matmul_kernel,
            count,
            pieces,
            cells,
            local,
            part,
            planes,
            acc is not None,
            token is not None,
            buffers,
        ),
        out_shape=out_shape,
        in_specs=[scalar, scalar] + [pl.BlockSpec(memory_space=pl.ANY)] * len(operands),
        out_specs=vmem(len(out_shape)),
        scratch_shapes=[
            pltpu.VMEM((buffers, rows, 2 * local), jnp.bfloat16),
            pltpu.SemaphoreType.DMA((buffers,)),
            pltpu.VMEM((count, padded, 2 * local), jnp.bfloat16),
            pltpu.VMEM((height, padded) if part else small, jnp.float32),
            pltpu.SemaphoreType.DMA(((2 * count + 2) * pieces,)),
            pltpu.VMEM(state.shape if part else small, jnp.bfloat16),
        ]
        + [pltpu.VMEM(block, jnp.bfloat16)] * (2 * count),
        compiler_params=params(),
        cost_estimate=cost(size),
        name="collide",
    )(jnp.stack(chips).astype(jnp.int32), core.astype(jnp.int32)[None], *operands)


def stream_kernel(part, shape, final, _, speed_ref, inflow_ref, code_ref, *refs):
    planes, height, depth, local = shape
    refs = list(refs)
    plane_refs = [refs.pop(0) for _ in range(planes + 2)]
    done = [refs.pop(0) for _ in range(2 if final else 1)] if part[0] > 0 else None
    out_ref = refs.pop(0)
    first, end = part
    full = local // LANES
    size = height * depth
    cells = planes * size
    half = cells // 2

    def tile(t, tail):
        def plane(x, y):
            at = t * size + y % height * depth
            return plane_refs[x + 1][rows_at(at, depth), :].astype(jnp.float32)

        speed = [speed_ref[first + t, d : d + 1, :] for d in range(3)]
        fast = [jnp.abs(s) for s in speed]
        up = [s > 0 for s in speed]
        inflow = inflow_ref[first + t, 0:1, :]
        for x in range(planes):
            for y in range(height):
                field = plane(x, y)
                total = field
                for d in range(3):
                    if d == 0:
                        lower, upper = plane(x - 1, y), plane(x + 1, y)
                    elif d == 1:
                        lower, upper = plane(x, y - 1), plane(x, y + 1)
                    else:
                        lower = pltpu.roll(field, 1, 0)
                        upper = pltpu.roll(field, depth - 1, 0)
                    near = jnp.where(up[d], lower, upper)
                    total = total - fast[d] * (field - near)
                at = (x * height + y) * depth
                here = slice(at, at + depth)
                code = code_ref[here, :]
                total = jnp.where(code == 0, total, jnp.where(code == 1, inflow, 0.0))
                total = total.astype(jnp.bfloat16)
                if final:
                    wide = total.astype(jnp.float32)
                    if tail:
                        out_ref[here, full * LANES : local] = total[:, :HALF]
                        lane = lax.broadcasted_iota(jnp.int32, wide.shape, 1)
                        wide = jnp.where(lane < HALF, wide, 0.0)
                    else:
                        lanes = pl.ds(pl.multiple_of((place + t) * LANES, LANES), LANES)
                        out_ref[here, lanes] = total
                    refs[0][here, :] += wide
                elif tail:
                    side = 0 if at < half else 1
                    to = t * cells + at - side * half
                    out_ref[to : to + depth, side * HALF : (side + 1) * HALF] = total[:, :HALF]
                else:
                    out_ref[rows_at(t * cells + at, depth), :] = total

    place = 0
    if not final:
        refs[0][...] = jnp.zeros_like(refs[0])
    if final:
        if done is None:
            refs[0][...] = jnp.zeros_like(refs[0])
        else:
            place = first
            out_ref[:, 0 : first * LANES] = done[0][...]
            refs[0][...] = done[1][...]

    def body(t, carry):
        tile(t, False)
        return carry

    lax.fori_loop(0, min(end, full) - first, body, 0)
    if end > full:
        tile(full - first, True)
        if final:
            refs[0][:, 0:1] = jnp.sum(refs[0][...], axis=1, keepdims=True)


def stream(part, planes, speed, inflow, code, shape, final, done, token):
    cells, local = shape[0] * shape[1] * shape[2], shape[3]
    operands = [token, speed, inflow, code, *planes, *done]
    if final:
        width = min(part[1] * LANES, local)
        out_shape = [
            jax.ShapeDtypeStruct((cells, width), jnp.bfloat16),
            jax.ShapeDtypeStruct((cells, LANES), jnp.float32),
        ]
    else:
        rows = packed_rows(*part, cells, local)
        out_shape = [
            jax.ShapeDtypeStruct((rows, LANES), jnp.bfloat16),
            jax.ShapeDtypeStruct((8, LANES), jnp.float32),
        ]
    return pl.pallas_call(
        functools.partial(stream_kernel, part, shape, final),
        out_shape=out_shape,
        in_specs=vmem(len(operands)),
        out_specs=vmem(len(out_shape)),
        compiler_params=params(),
        cost_estimate=cost(STREAM_COST),
        name="stream",
    )(*operands)


NEAR = ((0, 1), (1, 0), (2, 3), (3, 2))
FAR = ((0, 3), (3, 0), (1, 2), (2, 1))
RELAY = ((0, 2), (3, 1), (2, 3), (1, 0))
TWO = ((0, 2), (2, 0), (1, 3), (3, 1))


def along(block, pairs):
    perm = [(2 * a + c, 2 * b + c) for a, b in pairs for c in range(2)]
    return lax.ppermute(block, "vel", perm)


def other_core(block):
    return lax.ppermute(block, "vel", [(i, i ^ 1) for i in range(8)])


def line_sum(part):
    part = part + other_core(part)
    others = [along(part, pairs) for pairs in (NEAR, TWO, FAR)]
    return part + (others[0] + (others[1] + others[2]))


def tied(*values):
    return lax.optimization_barrier(values)


def line(deviation, collision, vel_order, inflow_value, wall_flag, inflow_flag):
    shape = deviation.shape
    planes, height, depth, local = shape
    cells = planes * height * depth
    parts = part_tiles(local)
    index = lax.axis_index("vel")
    chip, core = index // 2, index % 2
    middle = (chip == 1) | (chip == 2)
    tiles = local // LANES + 1

    def by_tile(rows):
        rows = jnp.pad(rows, ((0, 0), (0, tiles * LANES - local)))
        return rows.reshape(-1, tiles, LANES).transpose(1, 0, 2)

    speed = by_tile(jnp.stack(speeds(vel_order)))
    inflow = by_tile(inflow_value[None, :].astype(jnp.float32))
    code = jnp.where(wall_flag == 1, 2, inflow_flag).reshape(-1, 1)
    forward, backward = ring("space")

    def halo(relaxed):
        low = lax.ppermute(relaxed[-1], "space", forward)
        high = lax.ppermute(relaxed[0], "space", backward)
        return [low, *relaxed, high]

    def pair(blocks):
        return blocks, [other_core(block) for block in blocks]

    start, speed, inflow, code = tied(chip, speed, inflow, code)
    state = pack(deviation)
    for step in range(ITERS):
        final = step == ITERS - 1
        sent = [(along(block, FAR), along(block, NEAR)) for block in state]
        far, near = [f for f, _ in sent], [n for _, n in sent]
        far[0], near[0], start = tied(far[0], near[0], start)
        acc = matmul([pair(state)], [start], core, collision, cells, size=4 * collision.size)[0]
        *both, acc = tied(*far[1:], *near[1:], acc)
        far, near = far[:1] + both[: len(far) - 1], near[:1] + both[len(far) - 1 :]
        rest = jnp.where(middle, jnp.concatenate(far), jnp.concatenate(state))
        rest = along(rest, RELAY)
        acc = matmul([pair(near), pair(far)], [chip ^ 1, chip ^ 3], core, collision, cells, acc)[0]
        rest, acc = tied(rest, acc)
        rest = pair([rest])
        chunks, token = [], None
        for part, block in zip(parts, state):
            *relaxed, token = matmul(
                [rest], [chip ^ 2], core, collision, cells, acc, part, block, planes, token
            )
            chunks.append(halo(relaxed))
        state, done = [], ()
        for part, chunk in zip(parts, chunks):
            result = stream(part, chunk, speed, inflow, code, shape, final, done, token)
            state.append(result[0])
            done = tuple(result) if final else (result[1],)
    partial_sum = done[1][:, 0].reshape(planes, height, depth)
    return state[-1].reshape(shape), line_sum(partial_sum) / jnp.sqrt(jnp.float32(V))


def shards(deviation, collision, *rest):
    planes, _, depth, local = deviation.shape
    fits = local % LANES == HALF and planes % 2 == 0 and depth % 16 == 0 and local > PARTS[-1] * LANES
    body = line if lax.axis_size("vel") == 8 and fits else plain
    return body(deviation, collision, *rest)


def solution(mesh):
    placed = (
        P("space", None, None, "vel"),
        P("vel", None),
        P("vel"),
        P("vel"),
        P("space", None, None),
        P("space", None, None),
    )
    return jax.shard_map(
        shards,
        mesh=mesh,
        in_specs=placed,
        out_specs=(P("space", None, None, "vel"), P("space", None, None)),
        check_vma=False,
    )
```

```python
import functools

import jax
import jax.numpy as jnp
from jax import lax
from jax.experimental import pallas as pl
from jax.experimental.pallas import tpu as pltpu
from jax.sharding import PartitionSpec as P

NV = 24
V = 13824
ITERS = 2
LANES = 128
HALF = LANES // 2
COST = 1024
STREAM_COST = 1024
VMEM_LIMIT = 36 * 1024 * 1024
BUFFERS = 3


def speeds(vel_order):
    kx = vel_order // (NV * NV)
    ky = vel_order // NV % NV
    kz = vel_order % NV
    scale = 0.9 / (1.5 * (NV - 1))
    half = (NV - 1) / 2.0
    return [(k.astype(jnp.float32) - half) * scale for k in (kx, ky, kz)]


def ring(axis):
    count = lax.axis_size(axis)
    forward = [(i, (i + 1) % count) for i in range(count)]
    return forward, [(target, source) for source, target in forward]


def plain_step(state, collision, speed_list, inflow_value, wall_flag, inflow_flag):
    shape = state.shape
    cells = shape[0] * shape[1] * shape[2]
    local_vel = shape[3]
    flat = state.reshape(cells, local_vel)
    gathered = lax.all_gather(flat, "vel")
    gathered = gathered.transpose(1, 0, 2).reshape(cells, collision.shape[1])
    image = lax.dot_general(
        gathered, collision, (((1,), (1,)), ((), ())), preferred_element_type=jnp.float32
    )
    relaxed = (0.5 * flat.astype(jnp.float32) + 0.5 * image).astype(jnp.bfloat16).reshape(shape)
    forward, backward = ring("space")
    low = lax.ppermute(relaxed[-1:], "space", forward)
    high = lax.ppermute(relaxed[:1], "space", backward)
    padded = jnp.concatenate([low, relaxed, high], axis=0).astype(jnp.float32)
    field = padded[1:-1]
    total = field
    for axis, speed in enumerate(speed_list):
        if axis == 0:
            lower, upper = padded[:-2], padded[2:]
        else:
            lower, upper = jnp.roll(field, 1, axis=axis), jnp.roll(field, -1, axis=axis)
        total = total - jnp.where(speed > 0, speed * (field - lower), speed * (upper - field))
    total = jnp.where(inflow_flag[..., None] == 1, inflow_value.astype(jnp.float32), total)
    total = jnp.where(wall_flag[..., None] == 1, 0.0, total)
    return total.astype(jnp.bfloat16)


def plain(deviation, collision, vel_order, inflow_value, wall_flag, inflow_flag):
    state = deviation
    for _ in range(ITERS):
        state = plain_step(
            state, collision, speeds(vel_order), inflow_value, wall_flag, inflow_flag
        )
    partial_sum = jnp.sum(state.astype(jnp.float32), axis=3)
    return state, lax.psum(partial_sum, "vel") / jnp.sqrt(jnp.float32(V))


PARTS = ((6,), (8,))
BLOCKS = (3, 6)


def vmem(count):
    return [pl.BlockSpec(memory_space=pltpu.VMEM)] * count


def params():
    return pltpu.CompilerParams(vmem_limit_bytes=VMEM_LIMIT)


def cost(size=COST):
    return pl.CostEstimate(flops=size, bytes_accessed=size, transcendentals=0)


def rows_at(start, size):
    return pl.ds(pl.multiple_of(start, 16), size)


def spans(cuts, local):
    cuts = (0, *cuts, local // LANES + 1)
    return list(zip(cuts[:-1], cuts[1:]))


def blocks_of(part, local):
    return [span for span in spans(BLOCKS, local) if part[0] <= span[0] < part[1]]


def packed_rows(first, end, cells, local):
    return (end - first) * cells - (cells // 2 if end * LANES > local else 0)


def pack_kernel(deviation_ref, *outs):
    planes, height, depth, local = deviation_ref.shape
    cells = planes * height * depth
    half = cells // 2
    full = local // LANES
    for (first, end), out_ref in zip(spans((), local), outs):
        for x in range(planes):
            for y in range(height):
                at = (x * height + y) * depth
                for t in range(first, min(end, full)):
                    to = (t - first) * cells + at
                    out_ref[to : to + depth, :] = deviation_ref[
                        x, y, :, t * LANES : (t + 1) * LANES
                    ]
                if end > full:
                    side = 0 if at < half else 1
                    to = (full - first) * cells + at - side * half
                    out_ref[to : to + depth, side * HALF : (side + 1) * HALF] = deviation_ref[
                        x, y, :, full * LANES : local
                    ]


def pack(deviation):
    planes, height, depth, local = deviation.shape
    cells = planes * height * depth
    out_shape = [
        jax.ShapeDtypeStruct((packed_rows(*part, cells, local), LANES), jnp.bfloat16)
        for part in spans((), local)
    ]
    return pl.pallas_call(
        pack_kernel,
        out_shape=out_shape,
        in_specs=vmem(1),
        out_specs=vmem(len(out_shape)),
        compiler_params=params(),
        cost_estimate=cost(),
        name="pack",
    )(deviation)


def row_block(rows):
    return max(b for b in range(16, 577, 16) if rows % b == 0)


def unpack(own_ref, other_ref, first_core, whole_ref, k, cells, local):
    full = local // LANES
    half = cells // 2

    def tile(t, size=cells):
        own, other = own_ref[t * cells : t * cells + size], other_ref[t * cells : t * cells + size]
        return jnp.where(first_core, own, other), jnp.where(first_core, other, own)

    tiles = [tile(t) for t in range(full)]
    ends = tile(full, half)
    ends = [jnp.concatenate([e[:, :HALF], e[:, HALF:]], axis=0) for e in ends]
    for t in range(full):
        whole_ref[k, 0:cells, t * LANES : (t + 1) * LANES] = tiles[t][0]
    middle = jnp.concatenate([ends[0], tiles[0][1][:, :HALF]], axis=1)
    whole_ref[k, 0:cells, full * LANES : (full + 1) * LANES] = middle
    for t in range(full):
        right = tiles[t + 1][1][:, :HALF] if t + 1 < full else ends[1]
        both = jnp.concatenate([tiles[t][1][:, HALF:], right], axis=1)
        at = (full + 1 + t) * LANES
        whole_ref[k, 0:cells, at : at + LANES] = both


def matmul_kernel(
    count, pieces, cells, local, part, planes, has_acc, has_token, buffers, chips_ref, core_ref, *refs
):
    refs = list(refs)
    given = [[refs.pop(0) for _ in range(pieces)] for _ in range(2 * count)]
    collision_ref = refs.pop(0)
    acc_ref = refs.pop(0) if has_acc else None
    state_ref = refs.pop(0) if part else None
    if has_token:
        refs.pop(0)
    outs = [refs.pop(0) for _ in range(planes if part else 1)]
    if part:
        token_ref = refs.pop(0)
        token_ref[...] = jnp.zeros_like(token_ref)
    buffer_ref, sems, whole_ref, total_ref, load_sems, state_there = refs[:6]
    blocks_ref = refs[6:]
    total_ref = total_ref if part else outs[0]
    first, end = part or (0, local // LANES + 1)
    height = total_ref.shape[0]
    rows = buffer_ref.shape[1]
    blocks = height // rows
    steps = blocks * count
    width = 2 * local

    def copy(n):
        columns = pl.ds(pl.multiple_of(chips_ref[n // blocks] * width, LANES), width)
        return pltpu.make_async_copy(
            collision_ref.at[rows_at(first * LANES + n % blocks * rows, rows), columns],
            buffer_ref.at[n % buffers],
            sems.at[n % buffers],
        )

    def load(sources, target, number):
        copies, start = [], 0
        for i, source in enumerate(sources):
            here = pl.ds(start, source.shape[0])
            copies.append(
                pltpu.make_async_copy(source, target.at[here], load_sems.at[number * pieces + i])
            )
            start += source.shape[0]
        for one in copies:
            one.start()
        return copies

    def wait(copies):
        for one in copies:
            one.wait()

    loads = [load(sources, blocks_ref[i], i) for i, sources in enumerate(given)]
    for n in range(min(buffers - 1, steps)):
        copy(n).start()
    if has_acc:
        old = acc_ref.at[first * LANES : first * LANES + height, :]
        loads.append(load([old], total_ref, len(given)))
    if part:
        state_copy = load([state_ref], state_there, len(given) + 1)

    first_core = core_ref[0] == 0
    if not has_acc:
        total_ref[...] = jnp.zeros_like(total_ref)
    for k in range(count):
        wait(loads[2 * k] + loads[2 * k + 1])
        unpack(blocks_ref[2 * k], blocks_ref[2 * k + 1], first_core, whole_ref, k, cells, local)
    if has_acc:
        wait(loads[-1])

    def step(n, carry):
        @pl.when(n + buffers - 1 < steps)
        def _():
            copy(n + buffers - 1).start()

        copy(n).wait()
        total_ref[rows_at(n % blocks * rows, rows), :] += lax.dot_general(
            buffer_ref[n % buffers],
            whole_ref[n // blocks],
            (((1,), (1,)), ((), ())),
            preferred_element_type=jnp.float32,
        )
        return carry

    lax.fori_loop(0, steps, step, 0)

    if part:
        wait(state_copy)
        size = cells // planes
        whole_tiles = height // LANES

        def relax(t, state, image, lanes):
            relaxed = 0.5 * state.astype(jnp.float32) + 0.5 * image.T[0:cells, :]
            relaxed = relaxed.astype(jnp.bfloat16)
            for x in range(planes):
                outs[x][rows_at(t * size, size), 0:lanes] = relaxed[x * size : (x + 1) * size, :]

        def relax_tile(t, carry):
            image = total_ref[rows_at(t * LANES, LANES), :]
            relax(t, state_there[rows_at(t * cells, cells), :], image, LANES)
            return carry

        lax.fori_loop(0, whole_tiles, relax_tile, 0)
        if height % LANES:
            last = state_there[whole_tiles * cells :, :]
            state = jnp.concatenate([last[:, :HALF], last[:, HALF:]], axis=0)
            relax(whole_tiles, state, total_ref[whole_tiles * LANES :, :], HALF)
            for out_ref in outs:
                out_ref[whole_tiles * size :, HALF:LANES] = jnp.zeros((size, HALF), jnp.bfloat16)


def matmul(
    pairs,
    chips,
    core,
    collision,
    cells,
    acc=None,
    part=None,
    state=None,
    planes=0,
    token=None,
    size=COST,
):
    local = collision.shape[0]
    height = local
    if part:
        height = min(part[1] * LANES, local) - part[0] * LANES
    rows = row_block(height)
    buffers = BUFFERS
    count, pieces = len(pairs), len(pairs[0][0])
    padded = -(-cells // LANES) * LANES
    given = [a for pair in pairs for block in pair for a in block]
    operands = given + [collision] + [a for a in (acc, state, token) if a is not None]
    if part:
        shape = ((part[1] - part[0]) * cells // planes, LANES)
        out_shape = [jax.ShapeDtypeStruct(shape, jnp.bfloat16)] * planes
        out_shape.append(jax.ShapeDtypeStruct((8, LANES), jnp.float32))
    else:
        out_shape = [jax.ShapeDtypeStruct((local, padded), jnp.float32)]
    scalar = pl.BlockSpec(memory_space=pltpu.SMEM)
    small = (16, LANES)
    block = (packed_rows(0, local // LANES + 1, cells, local), LANES)
    return pl.pallas_call(
        functools.partial(
            matmul_kernel,
            count,
            pieces,
            cells,
            local,
            part,
            planes,
            acc is not None,
            token is not None,
            buffers,
        ),
        out_shape=out_shape,
        in_specs=[scalar, scalar] + [pl.BlockSpec(memory_space=pl.ANY)] * len(operands),
        out_specs=vmem(len(out_shape)),
        scratch_shapes=[
            pltpu.VMEM((buffers, rows, 2 * local), jnp.bfloat16),
            pltpu.SemaphoreType.DMA((buffers,)),
            pltpu.VMEM((count, padded, 2 * local), jnp.bfloat16),
            pltpu.VMEM((height, padded) if part else small, jnp.float32),
            pltpu.SemaphoreType.DMA(((2 * count + 2) * pieces,)),
            pltpu.VMEM(state.shape if part else small, jnp.bfloat16),
        ]
        + [pltpu.VMEM(block, jnp.bfloat16)] * (2 * count),
        compiler_params=params(),
        cost_estimate=cost(size),
        name="collide",
    )(jnp.stack(chips).astype(jnp.int32), core.astype(jnp.int32)[None], *operands)


def stream_kernel(part, shape, final, _, speed_ref, inflow_ref, code_ref, *refs):
    planes, height, depth, local = shape
    refs = list(refs)
    plane_refs = [refs.pop(0) for _ in range(planes + 2)]
    done_ref = refs.pop(0) if part[0] > 0 else None
    first, end = part
    blocks = [part] if final else blocks_of(part, local)
    out_refs = [refs.pop(0) for _ in blocks]
    full = local // LANES
    size = height * depth
    cells = planes * size
    half = cells // 2

    def tile(t, tail, out_ref, begin):
        def plane(x, y):
            at = t * size + y % height * depth
            return plane_refs[x + 1][rows_at(at, depth), :].astype(jnp.float32)

        speed = [speed_ref[first + t, d : d + 1, :] for d in range(3)]
        fast = [jnp.abs(s) for s in speed]
        up = [s > 0 for s in speed]
        inflow = inflow_ref[first + t, 0:1, :]
        for x in range(planes):
            for y in range(height):
                field = plane(x, y)
                total = field
                for d in range(3):
                    if d == 0:
                        lower, upper = plane(x - 1, y), plane(x + 1, y)
                    elif d == 1:
                        lower, upper = plane(x, y - 1), plane(x, y + 1)
                    else:
                        lower = pltpu.roll(field, 1, 0)
                        upper = pltpu.roll(field, depth - 1, 0)
                    near = jnp.where(up[d], lower, upper)
                    total = total - fast[d] * (field - near)
                at = (x * height + y) * depth
                here = slice(at, at + depth)
                code = code_ref[here, :]
                total = jnp.where(code == 0, total, jnp.where(code == 1, inflow, 0.0))
                total = total.astype(jnp.bfloat16)
                if final and tail:
                    out_ref[here, full * LANES : local] = total[:, :HALF]
                elif final:
                    lanes = pl.ds(pl.multiple_of((first + t) * LANES, LANES), LANES)
                    out_ref[here, lanes] = total
                elif tail:
                    side = 0 if at < half else 1
                    to = (first + t - begin) * cells + at - side * half
                    out_ref[to : to + depth, side * HALF : (side + 1) * HALF] = total[:, :HALF]
                else:
                    out_ref[rows_at((first + t - begin) * cells + at, depth), :] = total

    if not final:
        refs[0][...] = jnp.zeros_like(refs[0])
    elif first > 0:
        out_refs[0][:, 0 : first * LANES] = done_ref[...]

    for (begin, stop), out_ref in zip(blocks, out_refs):

        def body(t, carry):
            tile(t, False, out_ref, begin)
            return carry

        lax.fori_loop(begin - first, min(stop, full) - first, body, 0)
        if stop > full:
            tile(full - first, True, out_ref, begin)


def stream(part, planes, speed, inflow, code, shape, final, done, token):
    cells, local = shape[0] * shape[1] * shape[2], shape[3]
    operands = [token, speed, inflow, code, *planes, *done]
    if final:
        width = min(part[1] * LANES, local)
        out_shape = [jax.ShapeDtypeStruct((cells, width), jnp.bfloat16)]
    else:
        out_shape = [
            jax.ShapeDtypeStruct((packed_rows(*span, cells, local), LANES), jnp.bfloat16)
            for span in blocks_of(part, local)
        ] + [jax.ShapeDtypeStruct((8, LANES), jnp.float32)]
    return pl.pallas_call(
        functools.partial(stream_kernel, part, shape, final),
        out_shape=out_shape,
        in_specs=vmem(len(operands)),
        out_specs=vmem(len(out_shape)),
        compiler_params=params(),
        cost_estimate=cost(STREAM_COST),
        name="stream",
    )(*operands)


NEAR = ((0, 1), (1, 0), (2, 3), (3, 2))
FAR = ((0, 3), (3, 0), (1, 2), (2, 1))
RELAY = ((0, 2), (3, 1), (2, 3), (1, 0))
TWO = ((0, 2), (2, 0), (1, 3), (3, 1))


def along(block, pairs):
    perm = [(2 * a + c, 2 * b + c) for a, b in pairs for c in range(2)]
    return lax.ppermute(block, "vel", perm)


def other_core(block):
    return lax.ppermute(block, "vel", [(i, i ^ 1) for i in range(8)])


def totals_kernel(
    parts, shape, speed_ref, inflow_ref, code_ref, *refs
):
    planes, height, depth, local = shape
    refs = list(refs)
    plane_refs = [[refs.pop(0) for _ in range(planes)] for _ in parts]
    sum_ref, forward_ref, backward_ref, token_ref, wide_ref, ends_ref, inflow_sum_ref = refs
    size = height * depth
    token_ref[...] = jnp.zeros_like(token_ref)
    wide_ref[...] = jnp.zeros_like(wide_ref)
    ends_ref[...] = jnp.zeros_like(ends_ref)
    inflow_sum_ref[...] = jnp.zeros_like(inflow_sum_ref)
    for (first, end), mine in zip(parts, plane_refs):

        def body(t, carry):
            def plane(x, y):
                at = t * size + y % height * depth
                return mine[x][rows_at(at, depth), :].astype(jnp.float32)

            speed = [speed_ref[first + t, d : d + 1, :] for d in range(3)]
            fast = [jnp.abs(s) for s in speed]
            up = [s > 0 for s in speed]
            rise, fall = jnp.where(up[0], fast[0], 0.0), jnp.where(up[0], 0.0, fast[0])
            stay = 1.0 - (fast[0] + fast[1] + fast[2])
            inflow_sum_ref[0:1, :] += inflow_ref[first + t, 0:1, :]
            for x in range(planes):
                for y in range(height):
                    field = plane(x, y)
                    total = stay * field
                    if x > 0:
                        total = total + rise * plane(x - 1, y)
                    if x < planes - 1:
                        total = total + fall * plane(x + 1, y)
                    near = jnp.where(up[1], plane(x, y - 1), plane(x, y + 1))
                    total = total + fast[1] * near
                    lower, upper = pltpu.roll(field, 1, 0), pltpu.roll(field, depth - 1, 0)
                    total = total + fast[2] * jnp.where(up[2], lower, upper)
                    at = (x * height + y) * depth
                    wide_ref[at : at + depth, :] += total
                    at = y * depth
                    if x == planes - 1:
                        ends_ref[0, at : at + depth, :] += rise * field
                    if x == 0:
                        ends_ref[1, at : at + depth, :] += fall * field
            return carry

        lax.fori_loop(0, end - first, body, 0)
    flowing = jnp.sum(inflow_sum_ref[0:1, :], axis=1, keepdims=True)
    total = jnp.sum(wide_ref[...], axis=1, keepdims=True)
    code = code_ref[...]
    sum_ref[...] = jnp.where(code == 0, total, jnp.where(code == 1, flowing, 0.0))
    forward_ref[...] = jnp.sum(ends_ref[0], axis=1, keepdims=True)
    backward_ref[...] = jnp.sum(ends_ref[1], axis=1, keepdims=True)


def totals(chunks, speed, inflow, code, shape, parts):
    planes, height, depth, _ = shape
    size = height * depth
    operands = [speed, inflow, code] + [a for chunk in chunks for a in chunk[1:-1]]
    part, ahead, behind, token = pl.pallas_call(
        functools.partial(totals_kernel, tuple(parts), shape),
        out_shape=[
            jax.ShapeDtypeStruct((planes * size, 1), jnp.float32),
            jax.ShapeDtypeStruct((size, 1), jnp.float32),
            jax.ShapeDtypeStruct((size, 1), jnp.float32),
            jax.ShapeDtypeStruct((8, LANES), jnp.float32),
        ],
        in_specs=vmem(len(operands)),
        out_specs=vmem(4),
        scratch_shapes=[
            pltpu.VMEM((planes * size, LANES), jnp.float32),
            pltpu.VMEM((2, size, LANES), jnp.float32),
            pltpu.VMEM((8, LANES), jnp.float32),
        ],
        compiler_params=params(),
        cost_estimate=cost(),
        name="totals",
    )(*operands)
    return token, part, ahead, behind


def density_of(part, ahead, behind, code, shape, first, second):
    planes, height, depth, _ = shape
    ahead, behind, _ = tied(ahead, behind, first)
    forward, backward = ring("space")
    low = lax.ppermute(ahead.reshape(1, height, depth), "space", forward)
    high = lax.ppermute(behind.reshape(1, height, depth), "space", backward)
    none = jnp.zeros((planes - 1, height, depth), jnp.float32)
    ends = jnp.concatenate([low, none]) + jnp.concatenate([none, high])
    free = code.reshape(planes, height, depth) == 0
    part = part.reshape(planes, height, depth) + jnp.where(free, ends, 0.0)
    part = part + other_core(part)
    part, _ = tied(part, second)
    others = [along(part, pairs) for pairs in (NEAR, TWO, FAR)]
    part = part + (others[0] + (others[1] + others[2]))
    return part / jnp.sqrt(jnp.float32(V))


def tied(*values):
    return lax.optimization_barrier(values)


def line(deviation, collision, vel_order, inflow_value, wall_flag, inflow_flag):
    shape = deviation.shape
    planes, height, depth, local = shape
    cells = planes * height * depth
    index = lax.axis_index("vel")
    chip, core = index // 2, index % 2
    middle = (chip == 1) | (chip == 2)
    tiles = local // LANES + 1

    def by_tile(rows):
        rows = jnp.pad(rows, ((0, 0), (0, tiles * LANES - local)))
        return rows.reshape(-1, tiles, LANES).transpose(1, 0, 2)

    speed = by_tile(jnp.stack(speeds(vel_order)))
    inflow = by_tile(inflow_value[None, :].astype(jnp.float32))
    code = jnp.where(wall_flag == 1, 2, inflow_flag).reshape(-1, 1)
    forward, backward = ring("space")

    def halo(relaxed):
        low = lax.ppermute(relaxed[-1], "space", forward)
        high = lax.ppermute(relaxed[0], "space", backward)
        return [low, *relaxed, high]

    def pair(blocks):
        return blocks, [other_core(block) for block in blocks]

    start, speed, inflow, code = tied(chip, speed, inflow, code)
    state = pack(deviation)
    for step in range(ITERS):
        final = step == ITERS - 1
        sent = [(along(block, FAR), along(block, NEAR)) for block in state]
        far, near = [f for f, _ in sent], [n for _, n in sent]
        parts = spans(PARTS[step], local)
        early = len(state) - 1
        if early:
            *far[:early], start = tied(*far[:early], start)
        acc = matmul([pair(state)], [start], core, collision, cells)[0]
        *both, acc = tied(*far[early:], *near, acc)
        far[early:], near = both[:1], both[1:]
        whole = jnp.concatenate(state)
        rest = along(jnp.where(middle, jnp.concatenate(far), whole), RELAY)
        acc = matmul([pair(near), pair(far)], [chip ^ 1, chip ^ 3], core, collision, cells, acc)[0]
        rest, acc = tied(rest, acc)
        rest = pair([rest])
        chunks, token, at = [], None, 0
        for part in parts:
            mine = whole[at : at + packed_rows(*part, cells, local)]
            at += mine.shape[0]
            *relaxed, token = matmul(
                [rest], [chip ^ 2], core, collision, cells, acc, part, mine, planes, token
            )
            chunks.append(halo(relaxed))
        if final:
            token, *sums = totals(chunks, speed, inflow, code, shape, parts)
        state, done, firsts = [], (), []
        for part, chunk in zip(parts, chunks):
            *blocks, last = stream(part, chunk, speed, inflow, code, shape, final, done, token)
            state += blocks
            firsts.append(last)
            done = (last,)
    density = density_of(*sums, code, shape, chunks[0][0], firsts[0])
    return last.reshape(shape), density


def shards(deviation, collision, *rest):
    planes, _, depth, local = deviation.shape
    fits = local % LANES == HALF and planes % 2 == 0 and depth % 16 == 0 and local > max(sum(PARTS, ())) * LANES
    body = line if lax.axis_size("vel") == 8 and fits else plain
    return body(deviation, collision, *rest)


def solution(mesh):
    placed = (
        P("space", None, None, "vel"),
        P("vel", None),
        P("vel"),
        P("vel"),
        P("space", None, None),
        P("space", None, None),
    )
    return jax.shard_map(
        shards,
        mesh=mesh,
        in_specs=placed,
        out_specs=(P("space", None, None, "vel"), P("space", None, None)),
        check_vma=False,
    )
```

```python
import functools

import jax
import jax.numpy as jnp
from jax import lax
from jax.experimental import pallas as pl
from jax.experimental.pallas import tpu as pltpu
from jax.sharding import PartitionSpec as P

NV = 24
V = 13824
ITERS = 2
LANES = 128
HALF = LANES // 2
COST = 1024
STREAM_COST = 1024
VMEM_LIMIT = 36 * 1024 * 1024
BUFFERS = 3


def speeds(vel_order):
    kx = vel_order // (NV * NV)
    ky = vel_order // NV % NV
    kz = vel_order % NV
    scale = 0.9 / (1.5 * (NV - 1))
    half = (NV - 1) / 2.0
    return [(k.astype(jnp.float32) - half) * scale for k in (kx, ky, kz)]


def ring(axis):
    count = lax.axis_size(axis)
    forward = [(i, (i + 1) % count) for i in range(count)]
    return forward, [(target, source) for source, target in forward]


def plain_step(state, collision, speed_list, inflow_value, wall_flag, inflow_flag):
    shape = state.shape
    cells = shape[0] * shape[1] * shape[2]
    local_vel = shape[3]
    flat = state.reshape(cells, local_vel)
    gathered = lax.all_gather(flat, "vel")
    gathered = gathered.transpose(1, 0, 2).reshape(cells, collision.shape[1])
    image = lax.dot_general(
        gathered, collision, (((1,), (1,)), ((), ())), preferred_element_type=jnp.float32
    )
    relaxed = (0.5 * flat.astype(jnp.float32) + 0.5 * image).astype(jnp.bfloat16).reshape(shape)
    forward, backward = ring("space")
    low = lax.ppermute(relaxed[-1:], "space", forward)
    high = lax.ppermute(relaxed[:1], "space", backward)
    padded = jnp.concatenate([low, relaxed, high], axis=0).astype(jnp.float32)
    field = padded[1:-1]
    total = field
    for axis, speed in enumerate(speed_list):
        if axis == 0:
            lower, upper = padded[:-2], padded[2:]
        else:
            lower, upper = jnp.roll(field, 1, axis=axis), jnp.roll(field, -1, axis=axis)
        total = total - jnp.where(speed > 0, speed * (field - lower), speed * (upper - field))
    total = jnp.where(inflow_flag[..., None] == 1, inflow_value.astype(jnp.float32), total)
    total = jnp.where(wall_flag[..., None] == 1, 0.0, total)
    return total.astype(jnp.bfloat16)


def plain(deviation, collision, vel_order, inflow_value, wall_flag, inflow_flag):
    state = deviation
    for _ in range(ITERS):
        state = plain_step(
            state, collision, speeds(vel_order), inflow_value, wall_flag, inflow_flag
        )
    partial_sum = jnp.sum(state.astype(jnp.float32), axis=3)
    return state, lax.psum(partial_sum, "vel") / jnp.sqrt(jnp.float32(V))


PARTS = ((6,), (8,))
BLOCKS = (3, 6)


def vmem(count):
    return [pl.BlockSpec(memory_space=pltpu.VMEM)] * count


def params():
    return pltpu.CompilerParams(vmem_limit_bytes=VMEM_LIMIT)


def cost(size=COST):
    return pl.CostEstimate(flops=size, bytes_accessed=size, transcendentals=0)


def rows_at(start, size):
    return pl.ds(pl.multiple_of(start, 16), size)


def spans(cuts, local):
    cuts = (0, *cuts, local // LANES + 1)
    return list(zip(cuts[:-1], cuts[1:]))


def blocks_of(part, local):
    return [span for span in spans(BLOCKS, local) if part[0] <= span[0] < part[1]]


def packed_rows(first, end, cells, local):
    return (end - first) * cells - (cells // 2 if end * LANES > local else 0)


def pack_kernel(deviation_ref, *outs):
    planes, height, depth, local = deviation_ref.shape
    cells = planes * height * depth
    half = cells // 2
    full = local // LANES
    for (first, end), out_ref in zip(spans((), local), outs):
        for x in range(planes):
            for y in range(height):
                at = (x * height + y) * depth
                for t in range(first, min(end, full)):
                    to = (t - first) * cells + at
                    out_ref[to : to + depth, :] = deviation_ref[
                        x, y, :, t * LANES : (t + 1) * LANES
                    ]
                if end > full:
                    side = 0 if at < half else 1
                    to = (full - first) * cells + at - side * half
                    out_ref[to : to + depth, side * HALF : (side + 1) * HALF] = deviation_ref[
                        x, y, :, full * LANES : local
                    ]


def pack(deviation):
    planes, height, depth, local = deviation.shape
    cells = planes * height * depth
    out_shape = [
        jax.ShapeDtypeStruct((packed_rows(*part, cells, local), LANES), jnp.bfloat16)
        for part in spans((), local)
    ]
    return pl.pallas_call(
        pack_kernel,
        out_shape=out_shape,
        in_specs=vmem(1),
        out_specs=vmem(len(out_shape)),
        compiler_params=params(),
        cost_estimate=cost(),
        name="pack",
    )(deviation)


def row_block(rows):
    return max(b for b in range(16, 577, 16) if rows % b == 0)


def unpack(own_ref, other_ref, first_core, whole_ref, k, cells, local):
    full = local // LANES
    half = cells // 2

    def tile(t, size=cells):
        own, other = own_ref[t * cells : t * cells + size], other_ref[t * cells : t * cells + size]
        return jnp.where(first_core, own, other), jnp.where(first_core, other, own)

    tiles = [tile(t) for t in range(full)]
    ends = tile(full, half)
    ends = [jnp.concatenate([e[:, :HALF], e[:, HALF:]], axis=0) for e in ends]
    for t in range(full):
        whole_ref[k, 0:cells, t * LANES : (t + 1) * LANES] = tiles[t][0]
    middle = jnp.concatenate([ends[0], tiles[0][1][:, :HALF]], axis=1)
    whole_ref[k, 0:cells, full * LANES : (full + 1) * LANES] = middle
    for t in range(full):
        right = tiles[t + 1][1][:, :HALF] if t + 1 < full else ends[1]
        both = jnp.concatenate([tiles[t][1][:, HALF:], right], axis=1)
        at = (full + 1 + t) * LANES
        whole_ref[k, 0:cells, at : at + LANES] = both


def matmul_kernel(
    count, pieces, cells, local, part, planes, has_acc, has_token, buffers, chips_ref, core_ref, *refs
):
    refs = list(refs)
    given = [[refs.pop(0) for _ in range(n)] for n in pieces]
    collision_ref = refs.pop(0)
    acc_ref = refs.pop(0) if has_acc else None
    state_ref = refs.pop(0) if part else None
    if has_token:
        refs.pop(0)
    outs = [refs.pop(0) for _ in range(planes if part else 1)]
    if part:
        token_ref = refs.pop(0)
        token_ref[...] = jnp.zeros_like(token_ref)
    buffer_ref, sems, whole_ref, total_ref, load_sems, state_there = refs[:6]
    blocks_ref = refs[6:]
    total_ref = total_ref if part else outs[0]
    first, end = part or (0, local // LANES + 1)
    height = total_ref.shape[0]
    rows = buffer_ref.shape[1]
    blocks = height // rows
    steps = blocks * count
    width = 2 * local

    def copy(n):
        columns = pl.ds(pl.multiple_of(chips_ref[n // blocks] * width, LANES), width)
        return pltpu.make_async_copy(
            collision_ref.at[rows_at(first * LANES + n % blocks * rows, rows), columns],
            buffer_ref.at[n % buffers],
            sems.at[n % buffers],
        )

    most = max(pieces)

    def load(sources, target, number):
        copies, start = [], 0
        for i, source in enumerate(sources):
            here = pl.ds(start, source.shape[0])
            copies.append(
                pltpu.make_async_copy(source, target.at[here], load_sems.at[number * most + i])
            )
            start += source.shape[0]
        for one in copies:
            one.start()
        return copies

    def wait(copies):
        for one in copies:
            one.wait()

    loads = [load(sources, blocks_ref[i], i) for i, sources in enumerate(given)]
    for n in range(min(buffers - 1, steps)):
        copy(n).start()
    if has_acc:
        old = acc_ref.at[first * LANES : first * LANES + height, :]
        loads.append(load([old], total_ref, len(given)))
    if part:
        state_copy = load([state_ref], state_there, len(given) + 1)

    first_core = core_ref[0] == 0
    if not has_acc:
        total_ref[...] = jnp.zeros_like(total_ref)
    for k in range(count):
        wait(loads[2 * k] + loads[2 * k + 1])
        unpack(blocks_ref[2 * k], blocks_ref[2 * k + 1], first_core, whole_ref, k, cells, local)
    if has_acc:
        wait(loads[-1])

    def step(n, carry):
        @pl.when(n + buffers - 1 < steps)
        def _():
            copy(n + buffers - 1).start()

        copy(n).wait()
        total_ref[rows_at(n % blocks * rows, rows), :] += lax.dot_general(
            buffer_ref[n % buffers],
            whole_ref[n // blocks],
            (((1,), (1,)), ((), ())),
            preferred_element_type=jnp.float32,
        )
        return carry

    lax.fori_loop(0, steps, step, 0)

    if part:
        wait(state_copy)
        size = cells // planes
        whole_tiles = height // LANES

        def relax(t, state, image, lanes):
            relaxed = 0.5 * state.astype(jnp.float32) + 0.5 * image.T[0:cells, :]
            relaxed = relaxed.astype(jnp.bfloat16)
            for x in range(planes):
                outs[x][rows_at(t * size, size), 0:lanes] = relaxed[x * size : (x + 1) * size, :]

        def relax_tile(t, carry):
            image = total_ref[rows_at(t * LANES, LANES), :]
            relax(t, state_there[rows_at(t * cells, cells), :], image, LANES)
            return carry

        lax.fori_loop(0, whole_tiles, relax_tile, 0)
        if height % LANES:
            last = state_there[whole_tiles * cells :, :]
            state = jnp.concatenate([last[:, :HALF], last[:, HALF:]], axis=0)
            relax(whole_tiles, state, total_ref[whole_tiles * LANES :, :], HALF)
            for out_ref in outs:
                out_ref[whole_tiles * size :, HALF:LANES] = jnp.zeros((size, HALF), jnp.bfloat16)


def matmul(
    pairs,
    chips,
    core,
    collision,
    cells,
    acc=None,
    part=None,
    state=None,
    planes=0,
    token=None,
    size=COST,
):
    local = collision.shape[0]
    height = local
    if part:
        height = min(part[1] * LANES, local) - part[0] * LANES
    rows = row_block(height)
    buffers = BUFFERS
    count, pieces = len(pairs), tuple(len(block) for pair in pairs for block in pair)
    padded = -(-cells // LANES) * LANES
    given = [a for pair in pairs for block in pair for a in block]
    operands = given + [collision] + [a for a in (acc, state, token) if a is not None]
    if part:
        shape = ((part[1] - part[0]) * cells // planes, LANES)
        out_shape = [jax.ShapeDtypeStruct(shape, jnp.bfloat16)] * planes
        out_shape.append(jax.ShapeDtypeStruct((8, LANES), jnp.float32))
    else:
        out_shape = [jax.ShapeDtypeStruct((local, padded), jnp.float32)]
    scalar = pl.BlockSpec(memory_space=pltpu.SMEM)
    small = (16, LANES)
    block = (packed_rows(0, local // LANES + 1, cells, local), LANES)
    return pl.pallas_call(
        functools.partial(
            matmul_kernel,
            count,
            pieces,
            cells,
            local,
            part,
            planes,
            acc is not None,
            token is not None,
            buffers,
        ),
        out_shape=out_shape,
        in_specs=[scalar, scalar] + [pl.BlockSpec(memory_space=pl.ANY)] * len(operands),
        out_specs=vmem(len(out_shape)),
        scratch_shapes=[
            pltpu.VMEM((buffers, rows, 2 * local), jnp.bfloat16),
            pltpu.SemaphoreType.DMA((buffers,)),
            pltpu.VMEM((count, padded, 2 * local), jnp.bfloat16),
            pltpu.VMEM((height, padded) if part else small, jnp.float32),
            pltpu.SemaphoreType.DMA(((2 * count + 2) * max(pieces),)),
            pltpu.VMEM(state.shape if part else small, jnp.bfloat16),
        ]
        + [pltpu.VMEM(block, jnp.bfloat16)] * (2 * count),
        compiler_params=params(),
        cost_estimate=cost(size),
        name="collide",
    )(jnp.stack(chips).astype(jnp.int32), core.astype(jnp.int32)[None], *operands)


def stream_kernel(part, shape, final, _, speed_ref, inflow_ref, code_ref, *refs):
    planes, height, depth, local = shape
    refs = list(refs)
    plane_refs = [refs.pop(0) for _ in range(planes + 2)]
    done_ref = refs.pop(0) if part[0] > 0 else None
    first, end = part
    blocks = [part] if final else blocks_of(part, local)
    out_refs = [refs.pop(0) for _ in blocks]
    full = local // LANES
    size = height * depth
    cells = planes * size
    half = cells // 2

    def tile(t, tail, out_ref, begin):
        @functools.lru_cache
        def cell(x, y):
            at = t * size + y * depth
            return plane_refs[x + 1][rows_at(at, depth), :].astype(jnp.float32)

        def plane(x, y):
            return cell(x, y % height)

        speed = [speed_ref[first + t, d : d + 1, :] for d in range(3)]
        fast = [jnp.abs(s) for s in speed]
        up = [s > 0 for s in speed]
        inflow = inflow_ref[first + t, 0:1, :]
        for x in range(planes):
            for y in range(height):
                field = plane(x, y)
                total = field
                for d in range(3):
                    if d == 0:
                        lower, upper = plane(x - 1, y), plane(x + 1, y)
                    elif d == 1:
                        lower, upper = plane(x, y - 1), plane(x, y + 1)
                    else:
                        lower = pltpu.roll(field, 1, 0)
                        upper = pltpu.roll(field, depth - 1, 0)
                    near = jnp.where(up[d], lower, upper)
                    total = total - fast[d] * (field - near)
                at = (x * height + y) * depth
                here = slice(at, at + depth)
                code = code_ref[here, :]
                total = jnp.where(code == 0, total, jnp.where(code == 1, inflow, 0.0))
                total = total.astype(jnp.bfloat16)
                if final and tail:
                    out_ref[here, full * LANES : local] = total[:, :HALF]
                elif final:
                    lanes = pl.ds(pl.multiple_of((first + t) * LANES, LANES), LANES)
                    out_ref[here, lanes] = total
                elif tail:
                    side = 0 if at < half else 1
                    to = (first + t - begin) * cells + at - side * half
                    out_ref[to : to + depth, side * HALF : (side + 1) * HALF] = total[:, :HALF]
                else:
                    out_ref[rows_at((first + t - begin) * cells + at, depth), :] = total

    if not final:
        refs[0][...] = jnp.zeros_like(refs[0])
    elif first > 0:
        out_refs[0][:, 0 : first * LANES] = done_ref[...]

    for (begin, stop), out_ref in zip(blocks, out_refs):

        def body(t, carry):
            tile(t, False, out_ref, begin)
            return carry

        lax.fori_loop(begin - first, min(stop, full) - first, body, 0)
        if stop > full:
            tile(full - first, True, out_ref, begin)
    if not final and len(blocks) > 1:
        at = 0
        for ref in out_refs:
            refs[1][at : at + ref.shape[0], :] = ref[...]
            at += ref.shape[0]


def stream(part, planes, speed, inflow, code, shape, final, done, token):
    cells, local = shape[0] * shape[1] * shape[2], shape[3]
    operands = [token, speed, inflow, code, *planes, *done]
    if final:
        width = min(part[1] * LANES, local)
        out_shape = [jax.ShapeDtypeStruct((cells, width), jnp.bfloat16)]
    else:
        out_shape = [
            jax.ShapeDtypeStruct((packed_rows(*span, cells, local), LANES), jnp.bfloat16)
            for span in blocks_of(part, local)
        ] + [jax.ShapeDtypeStruct((8, LANES), jnp.float32)]
        if len(out_shape) > 2:
            rows = packed_rows(*part, cells, local)
            out_shape.append(jax.ShapeDtypeStruct((rows, LANES), jnp.bfloat16))
    return pl.pallas_call(
        functools.partial(stream_kernel, part, shape, final),
        out_shape=out_shape,
        in_specs=vmem(len(operands)),
        out_specs=vmem(len(out_shape)),
        compiler_params=params(),
        cost_estimate=cost(STREAM_COST),
        name="stream",
    )(*operands)


NEAR = ((0, 1), (1, 0), (2, 3), (3, 2))
FAR = ((0, 3), (3, 0), (1, 2), (2, 1))
RELAY = ((0, 2), (3, 1), (2, 3), (1, 0))
TWO = ((0, 2), (2, 0), (1, 3), (3, 1))


def along(block, pairs):
    perm = [(2 * a + c, 2 * b + c) for a, b in pairs for c in range(2)]
    return lax.ppermute(block, "vel", perm)


def other_core(block):
    return lax.ppermute(block, "vel", [(i, i ^ 1) for i in range(8)])


def totals_kernel(
    parts, shape, speed_ref, inflow_ref, code_ref, *refs
):
    planes, height, depth, local = shape
    refs = list(refs)
    plane_refs = [[refs.pop(0) for _ in range(planes)] for _ in parts]
    sum_ref, forward_ref, backward_ref, token_ref, wide_ref, ends_ref, inflow_sum_ref = refs
    size = height * depth
    token_ref[...] = jnp.zeros_like(token_ref)
    wide_ref[...] = jnp.zeros_like(wide_ref)
    ends_ref[...] = jnp.zeros_like(ends_ref)
    inflow_sum_ref[...] = jnp.zeros_like(inflow_sum_ref)
    for (first, end), mine in zip(parts, plane_refs):

        def body(t, carry):
            def plane(x, y):
                at = t * size + y % height * depth
                return mine[x][rows_at(at, depth), :].astype(jnp.float32)

            speed = [speed_ref[first + t, d : d + 1, :] for d in range(3)]
            fast = [jnp.abs(s) for s in speed]
            up = [s > 0 for s in speed]
            rise, fall = jnp.where(up[0], fast[0], 0.0), jnp.where(up[0], 0.0, fast[0])
            stay = 1.0 - (fast[0] + fast[1] + fast[2])
            inflow_sum_ref[0:1, :] += inflow_ref[first + t, 0:1, :]
            for x in range(planes):
                for y in range(height):
                    field = plane(x, y)
                    total = stay * field
                    if x > 0:
                        total = total + rise * plane(x - 1, y)
                    if x < planes - 1:
                        total = total + fall * plane(x + 1, y)
                    near = jnp.where(up[1], plane(x, y - 1), plane(x, y + 1))
                    total = total + fast[1] * near
                    lower, upper = pltpu.roll(field, 1, 0), pltpu.roll(field, depth - 1, 0)
                    total = total + fast[2] * jnp.where(up[2], lower, upper)
                    at = (x * height + y) * depth
                    wide_ref[at : at + depth, :] += total
                    at = y * depth
                    if x == planes - 1:
                        ends_ref[0, at : at + depth, :] += rise * field
                    if x == 0:
                        ends_ref[1, at : at + depth, :] += fall * field
            return carry

        lax.fori_loop(0, end - first, body, 0)
    flowing = jnp.sum(inflow_sum_ref[0:1, :], axis=1, keepdims=True)
    total = jnp.sum(wide_ref[...], axis=1, keepdims=True)
    code = code_ref[...]
    sum_ref[...] = jnp.where(code == 0, total, jnp.where(code == 1, flowing, 0.0))
    forward_ref[...] = jnp.sum(ends_ref[0], axis=1, keepdims=True)
    backward_ref[...] = jnp.sum(ends_ref[1], axis=1, keepdims=True)


def totals(chunks, speed, inflow, code, shape, parts):
    planes, height, depth, _ = shape
    size = height * depth
    operands = [speed, inflow, code] + [a for chunk in chunks for a in chunk[1:-1]]
    part, ahead, behind, token = pl.pallas_call(
        functools.partial(totals_kernel, tuple(parts), shape),
        out_shape=[
            jax.ShapeDtypeStruct((planes * size, 1), jnp.float32),
            jax.ShapeDtypeStruct((size, 1), jnp.float32),
            jax.ShapeDtypeStruct((size, 1), jnp.float32),
            jax.ShapeDtypeStruct((8, LANES), jnp.float32),
        ],
        in_specs=vmem(len(operands)),
        out_specs=vmem(4),
        scratch_shapes=[
            pltpu.VMEM((planes * size, LANES), jnp.float32),
            pltpu.VMEM((2, size, LANES), jnp.float32),
            pltpu.VMEM((8, LANES), jnp.float32),
        ],
        compiler_params=params(),
        cost_estimate=cost(),
        name="totals",
    )(*operands)
    return token, part, ahead, behind


def density_of(part, ahead, behind, code, shape, first, second):
    planes, height, depth, _ = shape
    ahead, behind, _ = tied(ahead, behind, first)
    forward, backward = ring("space")
    low = lax.ppermute(ahead.reshape(1, height, depth), "space", forward)
    high = lax.ppermute(behind.reshape(1, height, depth), "space", backward)
    none = jnp.zeros((planes - 1, height, depth), jnp.float32)
    ends = jnp.concatenate([low, none]) + jnp.concatenate([none, high])
    free = code.reshape(planes, height, depth) == 0
    part = part.reshape(planes, height, depth) + jnp.where(free, ends, 0.0)
    part = part + other_core(part)
    part, _ = tied(part, second)
    others = [along(part, pairs) for pairs in (NEAR, TWO, FAR)]
    part = part + (others[0] + (others[1] + others[2]))
    return part / jnp.sqrt(jnp.float32(V))


def tied(*values):
    return lax.optimization_barrier(values)


def line(deviation, collision, vel_order, inflow_value, wall_flag, inflow_flag):
    shape = deviation.shape
    planes, height, depth, local = shape
    cells = planes * height * depth
    index = lax.axis_index("vel")
    chip, core = index // 2, index % 2
    middle = (chip == 1) | (chip == 2)
    tiles = local // LANES + 1

    def by_tile(rows):
        rows = jnp.pad(rows, ((0, 0), (0, tiles * LANES - local)))
        return rows.reshape(-1, tiles, LANES).transpose(1, 0, 2)

    speed = by_tile(jnp.stack(speeds(vel_order)))
    inflow = by_tile(inflow_value[None, :].astype(jnp.float32))
    code = jnp.where(wall_flag == 1, 2, inflow_flag).reshape(-1, 1)
    forward, backward = ring("space")

    def halo(relaxed):
        low = lax.ppermute(relaxed[-1], "space", forward)
        high = lax.ppermute(relaxed[0], "space", backward)
        return [low, *relaxed, high]

    def pair(blocks):
        return blocks, [other_core(block) for block in blocks]

    start, speed, inflow, code = tied(chip, speed, inflow, code)
    blocks = state = pack(deviation)
    for step in range(ITERS):
        final = step == ITERS - 1
        far = [along(block, FAR) for block in blocks]
        near = [along(block, NEAR) for block in state]
        parts = spans(PARTS[step], local)
        early = len(blocks) - 1
        if early:
            *far[:early], start = tied(*far[:early], start)
        acc = matmul([pair(state)], [start], core, collision, cells)[0]
        *both, acc = tied(*far[early:], *near, acc)
        far[early:], near = both[:1], both[1:]
        whole = jnp.concatenate(state)
        rest = along(jnp.where(middle, jnp.concatenate(far), whole), RELAY)
        acc = matmul([pair(near), pair(far)], [chip ^ 1, chip ^ 3], core, collision, cells, acc)[0]
        rest, acc = tied(rest, acc)
        rest = pair([rest])
        chunks, token, at = [], None, 0
        for part in parts:
            mine = whole[at : at + packed_rows(*part, cells, local)]
            at += mine.shape[0]
            *relaxed, token = matmul(
                [rest], [chip ^ 2], core, collision, cells, acc, part, mine, planes, token
            )
            chunks.append(halo(relaxed))
        if final:
            token, *sums = totals(chunks, speed, inflow, code, shape, parts)
        blocks, state, done, firsts = [], [], (), []
        for part, chunk in zip(parts, chunks):
            result = list(stream(part, chunk, speed, inflow, code, shape, final, done, token))
            if not final:
                mine = [result.pop(0) for _ in blocks_of(part, local)]
                blocks += mine
                state.append(result[-1] if len(mine) > 1 else mine[0])
            firsts.append(result[0])
            done = (result[0],)
    density = density_of(*sums, code, shape, chunks[0][0], firsts[0])
    return done[0].reshape(shape), density


def shards(deviation, collision, *rest):
    planes, _, depth, local = deviation.shape
    fits = local % LANES == HALF and planes % 2 == 0 and depth % 16 == 0 and local > max(sum(PARTS, ())) * LANES
    body = line if lax.axis_size("vel") == 8 and fits else plain
    return body(deviation, collision, *rest)


def solution(mesh):
    placed = (
        P("space", None, None, "vel"),
        P("vel", None),
        P("vel"),
        P("vel"),
        P("space", None, None),
        P("space", None, None),
    )
    return jax.shard_map(
        shards,
        mesh=mesh,
        in_specs=placed,
        out_specs=(P("space", None, None, "vel"), P("space", None, None)),
        check_vma=False,
    )
```

```python
import functools

import jax
import jax.numpy as jnp
from jax import lax
from jax.experimental import pallas as pl
from jax.experimental.pallas import tpu as pltpu
from jax.sharding import PartitionSpec as P

NV = 24
V = 13824
ITERS = 2
LANES = 128
HALF = LANES // 2
COST = 1024
STREAM_COST = 1024
VMEM_LIMIT = 36 * 1024 * 1024
BUFFERS = 3


def speeds(vel_order):
    kx = vel_order // (NV * NV)
    ky = vel_order // NV % NV
    kz = vel_order % NV
    scale = 0.9 / (1.5 * (NV - 1))
    half = (NV - 1) / 2.0
    return [(k.astype(jnp.float32) - half) * scale for k in (kx, ky, kz)]


def ring(axis):
    count = lax.axis_size(axis)
    forward = [(i, (i + 1) % count) for i in range(count)]
    return forward, [(target, source) for source, target in forward]


def plain_step(state, collision, speed_list, inflow_value, wall_flag, inflow_flag):
    shape = state.shape
    cells = shape[0] * shape[1] * shape[2]
    local_vel = shape[3]
    flat = state.reshape(cells, local_vel)
    gathered = lax.all_gather(flat, "vel")
    gathered = gathered.transpose(1, 0, 2).reshape(cells, collision.shape[1])
    image = lax.dot_general(
        gathered, collision, (((1,), (1,)), ((), ())), preferred_element_type=jnp.float32
    )
    relaxed = (0.5 * flat.astype(jnp.float32) + 0.5 * image).astype(jnp.bfloat16).reshape(shape)
    forward, backward = ring("space")
    low = lax.ppermute(relaxed[-1:], "space", forward)
    high = lax.ppermute(relaxed[:1], "space", backward)
    padded = jnp.concatenate([low, relaxed, high], axis=0).astype(jnp.float32)
    field = padded[1:-1]
    total = field
    for axis, speed in enumerate(speed_list):
        if axis == 0:
            lower, upper = padded[:-2], padded[2:]
        else:
            lower, upper = jnp.roll(field, 1, axis=axis), jnp.roll(field, -1, axis=axis)
        total = total - jnp.where(speed > 0, speed * (field - lower), speed * (upper - field))
    total = jnp.where(inflow_flag[..., None] == 1, inflow_value.astype(jnp.float32), total)
    total = jnp.where(wall_flag[..., None] == 1, 0.0, total)
    return total.astype(jnp.bfloat16)


def plain(deviation, collision, vel_order, inflow_value, wall_flag, inflow_flag):
    state = deviation
    for _ in range(ITERS):
        state = plain_step(
            state, collision, speeds(vel_order), inflow_value, wall_flag, inflow_flag
        )
    partial_sum = jnp.sum(state.astype(jnp.float32), axis=3)
    return state, lax.psum(partial_sum, "vel") / jnp.sqrt(jnp.float32(V))


PARTS = ((6,), (8,))
BLOCKS = (3, 6)


def vmem(count):
    return [pl.BlockSpec(memory_space=pltpu.VMEM)] * count


def params():
    return pltpu.CompilerParams(vmem_limit_bytes=VMEM_LIMIT)


def cost(size=COST):
    return pl.CostEstimate(flops=size, bytes_accessed=size, transcendentals=0)


def rows_at(start, size):
    return pl.ds(pl.multiple_of(start, 16), size)


def spans(cuts, local):
    cuts = (0, *cuts, local // LANES + 1)
    return list(zip(cuts[:-1], cuts[1:]))


def blocks_of(part, local):
    return [span for span in spans(BLOCKS, local) if part[0] <= span[0] < part[1]]


def packed_rows(first, end, cells, local):
    return (end - first) * cells - (cells // 2 if end * LANES > local else 0)


def pack_kernel(deviation_ref, *outs):
    planes, height, depth, local = deviation_ref.shape
    cells = planes * height * depth
    half = cells // 2
    full = local // LANES
    for (first, end), out_ref in zip(spans((), local), outs):
        for x in range(planes):
            for y in range(height):
                at = (x * height + y) * depth
                for t in range(first, min(end, full)):
                    to = (t - first) * cells + at
                    out_ref[to : to + depth, :] = deviation_ref[
                        x, y, :, t * LANES : (t + 1) * LANES
                    ]
                if end > full:
                    side = 0 if at < half else 1
                    to = (full - first) * cells + at - side * half
                    out_ref[to : to + depth, side * HALF : (side + 1) * HALF] = deviation_ref[
                        x, y, :, full * LANES : local
                    ]


def pack(deviation):
    planes, height, depth, local = deviation.shape
    cells = planes * height * depth
    out_shape = [
        jax.ShapeDtypeStruct((packed_rows(*part, cells, local), LANES), jnp.bfloat16)
        for part in spans((), local)
    ]
    return pl.pallas_call(
        pack_kernel,
        out_shape=out_shape,
        in_specs=vmem(1),
        out_specs=vmem(len(out_shape)),
        compiler_params=params(),
        cost_estimate=cost(),
        name="pack",
    )(deviation)


def row_block(rows):
    return max(b for b in range(16, 577, 16) if rows % b == 0)


def unpack(own_ref, other_ref, first_core, whole_ref, k, cells, local):
    full = local // LANES
    half = cells // 2

    def tile(t, size=cells):
        own, other = own_ref[t * cells : t * cells + size], other_ref[t * cells : t * cells + size]
        return jnp.where(first_core, own, other), jnp.where(first_core, other, own)

    tiles = [tile(t) for t in range(full)]
    ends = tile(full, half)
    ends = [jnp.concatenate([e[:, :HALF], e[:, HALF:]], axis=0) for e in ends]
    for t in range(full):
        whole_ref[k, 0:cells, t * LANES : (t + 1) * LANES] = tiles[t][0]
    middle = jnp.concatenate([ends[0], tiles[0][1][:, :HALF]], axis=1)
    whole_ref[k, 0:cells, full * LANES : (full + 1) * LANES] = middle
    for t in range(full):
        right = tiles[t + 1][1][:, :HALF] if t + 1 < full else ends[1]
        both = jnp.concatenate([tiles[t][1][:, HALF:], right], axis=1)
        at = (full + 1 + t) * LANES
        whole_ref[k, 0:cells, at : at + LANES] = both


def matmul_kernel(
    count, pieces, cells, local, part, planes, has_acc, has_token, buffers, chips_ref, core_ref, *refs
):
    refs = list(refs)
    given = [[refs.pop(0) for _ in range(pieces)] for _ in range(2 * count)]
    collision_ref = refs.pop(0)
    acc_ref = refs.pop(0) if has_acc else None
    state_ref = refs.pop(0) if part else None
    if has_token:
        refs.pop(0)
    outs = [refs.pop(0) for _ in range(planes if part else 1)]
    if part:
        token_ref = refs.pop(0)
        token_ref[...] = jnp.zeros_like(token_ref)
    buffer_ref, sems, whole_ref, total_ref, load_sems, state_there = refs[:6]
    blocks_ref = refs[6:]
    total_ref = total_ref if part else outs[0]
    first, end = part or (0, local // LANES + 1)
    height = total_ref.shape[0]
    rows = buffer_ref.shape[1]
    blocks = height // rows
    steps = blocks * count
    width = 2 * local

    def copy(n):
        columns = pl.ds(pl.multiple_of(chips_ref[n // blocks] * width, LANES), width)
        return pltpu.make_async_copy(
            collision_ref.at[rows_at(first * LANES + n % blocks * rows, rows), columns],
            buffer_ref.at[n % buffers],
            sems.at[n % buffers],
        )

    def load(sources, target, number):
        copies, start = [], 0
        for i, source in enumerate(sources):
            here = pl.ds(start, source.shape[0])
            copies.append(
                pltpu.make_async_copy(source, target.at[here], load_sems.at[number * pieces + i])
            )
            start += source.shape[0]
        for one in copies:
            one.start()
        return copies

    def wait(copies):
        for one in copies:
            one.wait()

    loads = [load(sources, blocks_ref[i], i) for i, sources in enumerate(given)]
    for n in range(min(buffers - 1, steps)):
        copy(n).start()
    if has_acc:
        old = acc_ref.at[first * LANES : first * LANES + height, :]
        loads.append(load([old], total_ref, len(given)))
    if part:
        state_copy = load([state_ref], state_there, len(given) + 1)

    first_core = core_ref[0] == 0
    if not has_acc:
        total_ref[...] = jnp.zeros_like(total_ref)
    for k in range(count):
        wait(loads[2 * k] + loads[2 * k + 1])
        unpack(blocks_ref[2 * k], blocks_ref[2 * k + 1], first_core, whole_ref, k, cells, local)
    if has_acc:
        wait(loads[-1])

    def step(n, carry):
        @pl.when(n + buffers - 1 < steps)
        def _():
            copy(n + buffers - 1).start()

        copy(n).wait()
        total_ref[rows_at(n % blocks * rows, rows), :] += lax.dot_general(
            buffer_ref[n % buffers],
            whole_ref[n // blocks],
            (((1,), (1,)), ((), ())),
            preferred_element_type=jnp.float32,
        )
        return carry

    lax.fori_loop(0, steps, step, 0)

    if part:
        wait(state_copy)
        size = cells // planes
        whole_tiles = height // LANES

        def relax(t, state, image, lanes):
            relaxed = 0.5 * state.astype(jnp.float32) + 0.5 * image.T[0:cells, :]
            relaxed = relaxed.astype(jnp.bfloat16)
            for x in range(planes):
                outs[x][rows_at(t * size, size), 0:lanes] = relaxed[x * size : (x + 1) * size, :]

        def relax_tile(t, carry):
            image = total_ref[rows_at(t * LANES, LANES), :]
            relax(t, state_there[rows_at(t * cells, cells), :], image, LANES)
            return carry

        lax.fori_loop(0, whole_tiles, relax_tile, 0)
        if height % LANES:
            last = state_there[whole_tiles * cells :, :]
            state = jnp.concatenate([last[:, :HALF], last[:, HALF:]], axis=0)
            relax(whole_tiles, state, total_ref[whole_tiles * LANES :, :], HALF)
            for out_ref in outs:
                out_ref[whole_tiles * size :, HALF:LANES] = jnp.zeros((size, HALF), jnp.bfloat16)


def matmul(
    pairs,
    chips,
    core,
    collision,
    cells,
    acc=None,
    part=None,
    state=None,
    planes=0,
    token=None,
    size=COST,
):
    local = collision.shape[0]
    height = local
    if part:
        height = min(part[1] * LANES, local) - part[0] * LANES
    rows = row_block(height)
    buffers = BUFFERS
    count, pieces = len(pairs), len(pairs[0][0])
    padded = -(-cells // LANES) * LANES
    given = [a for pair in pairs for block in pair for a in block]
    operands = given + [collision] + [a for a in (acc, state, token) if a is not None]
    if part:
        shape = ((part[1] - part[0]) * cells // planes, LANES)
        out_shape = [jax.ShapeDtypeStruct(shape, jnp.bfloat16)] * planes
        out_shape.append(jax.ShapeDtypeStruct((8, LANES), jnp.float32))
    else:
        out_shape = [jax.ShapeDtypeStruct((local, padded), jnp.float32)]
    scalar = pl.BlockSpec(memory_space=pltpu.SMEM)
    small = (16, LANES)
    block = (packed_rows(0, local // LANES + 1, cells, local), LANES)
    return pl.pallas_call(
        functools.partial(
            matmul_kernel,
            count,
            pieces,
            cells,
            local,
            part,
            planes,
            acc is not None,
            token is not None,
            buffers,
        ),
        out_shape=out_shape,
        in_specs=[scalar, scalar] + [pl.BlockSpec(memory_space=pl.ANY)] * len(operands),
        out_specs=vmem(len(out_shape)),
        scratch_shapes=[
            pltpu.VMEM((buffers, rows, 2 * local), jnp.bfloat16),
            pltpu.SemaphoreType.DMA((buffers,)),
            pltpu.VMEM((count, padded, 2 * local), jnp.bfloat16),
            pltpu.VMEM((height, padded) if part else small, jnp.float32),
            pltpu.SemaphoreType.DMA(((2 * count + 2) * pieces,)),
            pltpu.VMEM(state.shape if part else small, jnp.bfloat16),
        ]
        + [pltpu.VMEM(block, jnp.bfloat16)] * (2 * count),
        compiler_params=params(),
        cost_estimate=cost(size),
        name="collide",
    )(jnp.stack(chips).astype(jnp.int32), core.astype(jnp.int32)[None], *operands)


def stream_kernel(part, shape, final, _, speed_ref, inflow_ref, code_ref, *refs):
    planes, height, depth, local = shape
    refs = list(refs)
    plane_refs = [refs.pop(0) for _ in range(planes + 2)]
    done_ref = refs.pop(0) if part[0] > 0 else None
    first, end = part
    blocks = [part] if final else blocks_of(part, local)
    out_refs = [refs.pop(0) for _ in blocks]
    full = local // LANES
    size = height * depth
    cells = planes * size
    half = cells // 2

    def tile(t, tail, out_ref, begin):
        def plane(x, y):
            at = t * size + y % height * depth
            return plane_refs[x + 1][rows_at(at, depth), :].astype(jnp.float32)

        speed = [speed_ref[first + t, d : d + 1, :] for d in range(3)]
        fast = [jnp.abs(s) for s in speed]
        up = [s > 0 for s in speed]
        inflow = inflow_ref[first + t, 0:1, :]
        for x in range(planes):
            for y in range(height):
                field = plane(x, y)
                total = field
                for d in range(3):
                    if d == 0:
                        lower, upper = plane(x - 1, y), plane(x + 1, y)
                    elif d == 1:
                        lower, upper = plane(x, y - 1), plane(x, y + 1)
                    else:
                        lower = pltpu.roll(field, 1, 0)
                        upper = pltpu.roll(field, depth - 1, 0)
                    near = jnp.where(up[d], lower, upper)
                    total = total - fast[d] * (field - near)
                at = (x * height + y) * depth
                here = slice(at, at + depth)
                code = code_ref[here, :]
                total = jnp.where(code == 0, total, jnp.where(code == 1, inflow, 0.0))
                total = total.astype(jnp.bfloat16)
                if final and tail:
                    out_ref[here, full * LANES : local] = total[:, :HALF]
                elif final:
                    lanes = pl.ds(pl.multiple_of((first + t) * LANES, LANES), LANES)
                    out_ref[here, lanes] = total
                elif tail:
                    side = 0 if at < half else 1
                    to = (first + t - begin) * cells + at - side * half
                    out_ref[to : to + depth, side * HALF : (side + 1) * HALF] = total[:, :HALF]
                else:
                    out_ref[rows_at((first + t - begin) * cells + at, depth), :] = total

    if not final:
        refs[0][...] = jnp.zeros_like(refs[0])
    elif first > 0:
        out_refs[0][:, 0 : first * LANES] = done_ref[...]

    for (begin, stop), out_ref in zip(blocks, out_refs):

        def body(t, carry):
            tile(t, False, out_ref, begin)
            return carry

        lax.fori_loop(begin - first, min(stop, full) - first, body, 0)
        if stop > full:
            tile(full - first, True, out_ref, begin)


def stream(part, planes, speed, inflow, code, shape, final, done, token):
    cells, local = shape[0] * shape[1] * shape[2], shape[3]
    operands = [token, speed, inflow, code, *planes, *done]
    if final:
        width = min(part[1] * LANES, local)
        out_shape = [jax.ShapeDtypeStruct((cells, width), jnp.bfloat16)]
    else:
        out_shape = [
            jax.ShapeDtypeStruct((packed_rows(*span, cells, local), LANES), jnp.bfloat16)
            for span in blocks_of(part, local)
        ] + [jax.ShapeDtypeStruct((8, LANES), jnp.float32)]
    return pl.pallas_call(
        functools.partial(stream_kernel, part, shape, final),
        out_shape=out_shape,
        in_specs=vmem(len(operands)),
        out_specs=vmem(len(out_shape)),
        compiler_params=params(),
        cost_estimate=cost(STREAM_COST),
        name="stream",
    )(*operands)


NEAR = ((0, 1), (1, 0), (2, 3), (3, 2))
FAR = ((0, 3), (3, 0), (1, 2), (2, 1))
RELAY = ((0, 2), (3, 1), (2, 3), (1, 0))
TWO = ((0, 2), (2, 0), (1, 3), (3, 1))


def along(block, pairs):
    perm = [(2 * a + c, 2 * b + c) for a, b in pairs for c in range(2)]
    return lax.ppermute(block, "vel", perm)


def other_core(block):
    return lax.ppermute(block, "vel", [(i, i ^ 1) for i in range(8)])


def totals_kernel(
    parts, shape, speed_ref, inflow_ref, code_ref, *refs
):
    planes, height, depth, local = shape
    refs = list(refs)
    plane_refs = [[refs.pop(0) for _ in range(planes)] for _ in parts]
    sum_ref, forward_ref, backward_ref, token_ref, wide_ref, ends_ref, inflow_sum_ref = refs
    size = height * depth
    token_ref[...] = jnp.zeros_like(token_ref)
    wide_ref[...] = jnp.zeros_like(wide_ref)
    ends_ref[...] = jnp.zeros_like(ends_ref)
    inflow_sum_ref[...] = jnp.zeros_like(inflow_sum_ref)
    for (first, end), mine in zip(parts, plane_refs):

        def body(t, carry):
            def plane(x, y):
                at = t * size + y % height * depth
                return mine[x][rows_at(at, depth), :].astype(jnp.float32)

            speed = [speed_ref[first + t, d : d + 1, :] for d in range(3)]
            fast = [jnp.abs(s) for s in speed]
            up = [s > 0 for s in speed]
            rise, fall = jnp.where(up[0], fast[0], 0.0), jnp.where(up[0], 0.0, fast[0])
            stay = 1.0 - (fast[0] + fast[1] + fast[2])
            inflow_sum_ref[0:1, :] += inflow_ref[first + t, 0:1, :]
            for x in range(planes):
                for y in range(height):
                    field = plane(x, y)
                    total = stay * field
                    if x > 0:
                        total = total + rise * plane(x - 1, y)
                    if x < planes - 1:
                        total = total + fall * plane(x + 1, y)
                    near = jnp.where(up[1], plane(x, y - 1), plane(x, y + 1))
                    total = total + fast[1] * near
                    lower, upper = pltpu.roll(field, 1, 0), pltpu.roll(field, depth - 1, 0)
                    total = total + fast[2] * jnp.where(up[2], lower, upper)
                    at = (x * height + y) * depth
                    wide_ref[at : at + depth, :] += total
                    at = y * depth
                    if x == planes - 1:
                        ends_ref[0, at : at + depth, :] += rise * field
                    if x == 0:
                        ends_ref[1, at : at + depth, :] += fall * field
            return carry

        lax.fori_loop(0, end - first, body, 0)
    flowing = jnp.sum(inflow_sum_ref[0:1, :], axis=1, keepdims=True)
    total = jnp.sum(wide_ref[...], axis=1, keepdims=True)
    code = code_ref[...]
    sum_ref[...] = jnp.where(code == 0, total, jnp.where(code == 1, flowing, 0.0))
    forward_ref[...] = jnp.sum(ends_ref[0], axis=1, keepdims=True)
    backward_ref[...] = jnp.sum(ends_ref[1], axis=1, keepdims=True)


def totals(chunks, speed, inflow, code, shape, parts):
    planes, height, depth, _ = shape
    size = height * depth
    operands = [speed, inflow, code] + [a for chunk in chunks for a in chunk[1:-1]]
    part, ahead, behind, token = pl.pallas_call(
        functools.partial(totals_kernel, tuple(parts), shape),
        out_shape=[
            jax.ShapeDtypeStruct((planes * size, 1), jnp.float32),
            jax.ShapeDtypeStruct((size, 1), jnp.float32),
            jax.ShapeDtypeStruct((size, 1), jnp.float32),
            jax.ShapeDtypeStruct((8, LANES), jnp.float32),
        ],
        in_specs=vmem(len(operands)),
        out_specs=vmem(4),
        scratch_shapes=[
            pltpu.VMEM((planes * size, LANES), jnp.float32),
            pltpu.VMEM((2, size, LANES), jnp.float32),
            pltpu.VMEM((8, LANES), jnp.float32),
        ],
        compiler_params=params(),
        cost_estimate=cost(),
        name="totals",
    )(*operands)
    return token, part, ahead, behind


def density_of(part, ahead, behind, code, shape, first, second):
    planes, height, depth, _ = shape
    ahead, behind, _ = tied(ahead, behind, first)
    forward, backward = ring("space")
    low = lax.ppermute(ahead.reshape(1, height, depth), "space", forward)
    high = lax.ppermute(behind.reshape(1, height, depth), "space", backward)
    none = jnp.zeros((planes - 1, height, depth), jnp.float32)
    ends = jnp.concatenate([low, none]) + jnp.concatenate([none, high])
    free = code.reshape(planes, height, depth) == 0
    part = part.reshape(planes, height, depth) + jnp.where(free, ends, 0.0)
    part = part + other_core(part)
    part, _ = tied(part, second)
    for pairs in (NEAR, TWO):
        part = part + along(part, pairs)
    return part / jnp.sqrt(jnp.float32(V))


def tied(*values):
    return lax.optimization_barrier(values)


def line(deviation, collision, vel_order, inflow_value, wall_flag, inflow_flag):
    shape = deviation.shape
    planes, height, depth, local = shape
    cells = planes * height * depth
    index = lax.axis_index("vel")
    chip, core = index // 2, index % 2
    middle = (chip == 1) | (chip == 2)
    tiles = local // LANES + 1

    def by_tile(rows):
        rows = jnp.pad(rows, ((0, 0), (0, tiles * LANES - local)))
        return rows.reshape(-1, tiles, LANES).transpose(1, 0, 2)

    speed = by_tile(jnp.stack(speeds(vel_order)))
    inflow = by_tile(inflow_value[None, :].astype(jnp.float32))
    code = jnp.where(wall_flag == 1, 2, inflow_flag).reshape(-1, 1)
    forward, backward = ring("space")

    def halo(relaxed):
        low = lax.ppermute(relaxed[-1], "space", forward)
        high = lax.ppermute(relaxed[0], "space", backward)
        return [low, *relaxed, high]

    def pair(blocks):
        return blocks, [other_core(block) for block in blocks]

    start, speed, inflow, code = tied(chip, speed, inflow, code)
    state = pack(deviation)
    for step in range(ITERS):
        final = step == ITERS - 1
        sent = [(along(block, FAR), along(block, NEAR)) for block in state]
        far, near = [f for f, _ in sent], [n for _, n in sent]
        parts = spans(PARTS[step], local)
        early = len(state) - 1
        if early:
            *far[:early], start = tied(*far[:early], start)
        acc = matmul([pair(state)], [start], core, collision, cells)[0]
        *both, acc = tied(*far[early:], *near, acc)
        far[early:], near = both[:1], both[1:]
        whole = jnp.concatenate(state)
        rest = along(jnp.where(middle, jnp.concatenate(far), whole), RELAY)
        acc = matmul([pair(near), pair(far)], [chip ^ 1, chip ^ 3], core, collision, cells, acc)[0]
        rest, acc = tied(rest, acc)
        rest = pair([rest])
        chunks, token, at = [], None, 0
        for part in parts:
            mine = whole[at : at + packed_rows(*part, cells, local)]
            at += mine.shape[0]
            *relaxed, token = matmul(
                [rest], [chip ^ 2], core, collision, cells, acc, part, mine, planes, token
            )
            chunks.append(halo(relaxed))
        if final:
            token, *sums = totals(chunks, speed, inflow, code, shape, parts)
        state, done, firsts = [], (), []
        for part, chunk in zip(parts, chunks):
            *blocks, last = stream(part, chunk, speed, inflow, code, shape, final, done, token)
            state += blocks
            firsts.append(last)
            done = (last,)
    density = density_of(*sums, code, shape, chunks[0][0], firsts[0])
    return last.reshape(shape), density


def shards(deviation, collision, *rest):
    planes, _, depth, local = deviation.shape
    fits = local % LANES == HALF and planes % 2 == 0 and depth % 16 == 0 and local > max(sum(PARTS, ())) * LANES
    body = line if lax.axis_size("vel") == 8 and fits else plain
    return body(deviation, collision, *rest)


def solution(mesh):
    placed = (
        P("space", None, None, "vel"),
        P("vel", None),
        P("vel"),
        P("vel"),
        P("space", None, None),
        P("space", None, None),
    )
    return jax.shard_map(
        shards,
        mesh=mesh,
        in_specs=placed,
        out_specs=(P("space", None, None, "vel"), P("space", None, None)),
        check_vma=False,
    )
```
